32 devices in a mesh: grp: 8 (over y, x, core), in: 4 (over z).
Axes of the slice: x: 2, y: 2, z: 4, core: 2. Of those that a mesh axis runs over, the one named last changes fastest.
Arguments:
- tokens: bfloat16 [4096, 1024], P(('grp', 'in')), may hold values from -6 to 6
- segments: int32 [32, 128], P(('grp', 'in')), may hold values from 0 to 2, never falling along the last dimension, each value on 1 to 64 neighbouring positions
- cotangent: bfloat16 [4096, 1024], P(('grp', 'in')), may hold values from -6 to 6
- vectors: float32 [12288], P('in'), may hold values from -0.5 to 1.5
- vector_moment: float32 [12288], P('in'), may hold values from -4 to 4
- qkv_weight: float32 [1024, 3072], P('in', 'grp'), may hold values from -0.1875 to 0.1875
- qkv_moment: float32 [1024, 3072], P('in', 'grp'), may hold values from -3 to 3
- qkv_left: float32 [1024, 1024], P('in', 'grp'), may hold values from -0.1 to 0.8, as said below
- qkv_right: float32 [3072, 3072], P('grp', 'in'), may hold values from -0.1 to 0.8, as said below
- qkv_left_root: float32 [1024, 1024], P('in', 'grp'), may hold values from -1 to 3
- qkv_right_root: float32 [3072, 3072], P('grp', 'in'), may hold values from -1 to 3
- out_weight: float32 [1024, 1024], P('in', 'grp'), may hold values from -0.5 to 0.5
- out_moment: float32 [1024, 1024], P('in', 'grp'), may hold values from -3 to 3
- out_left: float32 [1024, 1024], P('in', 'grp'), may hold values from -0.1 to 0.8, as said below
- out_right: float32 [1024, 1024], P('grp', 'in'), may hold values from -0.1 to 0.8, as said below
- out_left_root: float32 [1024, 1024], P('in', 'grp'), may hold values from -1 to 3
- out_right_root: float32 [1024, 1024], P('grp', 'in'), may hold values from -1 to 3
- fc_weight: float32 [1024, 4096], P('in', 'grp'), may hold values from -0.1875 to 0.1875
- fc_moment: float32 [1024, 4096], P('in', 'grp'), may hold values from -3 to 3
- fc_left: float32 [1024, 1024], P('in', 'grp'), may hold values from -0.1 to 0.8, as said below
- fc_right: float32 [4096, 4096], P('grp', 'in'), may hold values from -0.1 to 0.8, as said below
- fc_left_root: float32 [1024, 1024], P('in', 'grp'), may hold values from -1 to 3
- fc_right_root: float32 [4096, 4096], P('grp', 'in'), may hold values from -1 to 3
- proj_weight: float32 [4096, 1024], P('in', 'grp'), may hold values from -0.09375 to 0.09375
- proj_moment: float32 [4096, 1024], P('in', 'grp'), may hold values from -3 to 3
- proj_left: float32 [4096, 4096], P('in', 'grp'), may hold values from -0.1 to 0.8, as said below
- proj_right: float32 [1024, 1024], P('grp', 'in'), may hold values from -0.1 to 0.8, as said below
- proj_left_root: float32 [4096, 4096], P('in', 'grp'), may hold values from -1 to 3
- proj_right_root: float32 [1024, 1024], P('grp', 'in'), may hold values from -1 to 3
Outputs:
- output: bfloat16 [4096, 1024], P(('grp', 'in'))
- input_grad: bfloat16 [4096, 1024], P(('grp', 'in'))
- qkv_grad: float32 [1024, 3072], P('in', 'grp')
- qkv_left_new: float32 [1024, 1024], P('in', 'grp')
- qkv_right_new: float32 [3072, 3072], P('grp', 'in')
- qkv_moment_new: float32 [1024, 3072], P('in', 'grp')
- qkv_weight_new: float32 [1024, 3072], P('in', 'grp')
- qkv_copy: bfloat16 [1024, 3072], P('in', 'grp')
- out_grad: float32 [1024, 1024], P('in', 'grp')
- out_left_new: float32 [1024, 1024], P('in', 'grp')
- out_right_new: float32 [1024, 1024], P('grp', 'in')
- out_moment_new: float32 [1024, 1024], P('in', 'grp')
- out_weight_new: float32 [1024, 1024], P('in', 'grp')
- out_copy: bfloat16 [1024, 1024], P('in', 'grp')
- fc_grad: float32 [1024, 4096], P('in', 'grp')
- fc_left_new: float32 [1024, 1024], P('in', 'grp')
- fc_right_new: float32 [4096, 4096], P('grp', 'in')
- fc_moment_new: float32 [1024, 4096], P('in', 'grp')
- fc_weight_new: float32 [1024, 4096], P('in', 'grp')
- fc_copy: bfloat16 [1024, 4096], P('in', 'grp')
- proj_grad: float32 [4096, 1024], P('in', 'grp')
- proj_left_new: float32 [4096, 4096], P('in', 'grp')
- proj_right_new: float32 [1024, 1024], P('grp', 'in')
- proj_moment_new: float32 [4096, 1024], P('in', 'grp')
- proj_weight_new: float32 [4096, 1024], P('in', 'grp')
- proj_copy: bfloat16 [4096, 1024], P('in', 'grp')
- vector_grad: float32 [12288], P('in')
- vector_moment_new: float32 [12288], P('in')
- vectors_new: float32 [12288], P('in')
The draws below stay inside these ranges and needn't reach their ends.
Inputs may be any that keep to these rules, and one draw needn't show every extreme that they name: `segments`: segment numbers never fall along a sequence. `qkv_left`: Symmetric. `qkv_right`: Symmetric. `out_left`: Symmetric. `out_right`: Symmetric. `fc_left`: Symmetric. `fc_right`: Symmetric. `proj_left`: Symmetric. `proj_right`: Symmetric.
All inputs are finite; a program needn't handle non-finite values.
Results may differ from the reference program's by a relative error of at most 0.011.
The reference program's roundings to bfloat16 on the way count: a program that leaves them out, or rounds other values in their place, can miss the bound.
Values may be sent and summed in bfloat16 or wider, within the bound.
No kernel may reach another device: no remote copies, remote signals or barrier semaphores. Data moves between devices by JAX's collectives and lax.ppermute only.
A program may use at most 256 MiB of HBM per device.

```python
import functools
import math
import jax
import jax.numpy as jnp
import numpy as np
from jax import lax

D = 1024
FF = 4096
HEADS = 16
HEAD_DIM = 64
SEQ = 128
SEQS = 32
TOKENS = 4096
VEC = 12288


def statistic(key, order, salt):
    first, second = jax.random.split(jax.random.fold_in(key, 1000 + salt))
    diagonal = jax.random.uniform(first, (order,), jnp.float32, 0.05, 0.5)
    noise = jax.random.uniform(second, (order, order), jnp.float32, -1.0, 1.0) * (0.1 / math.sqrt(order))
    noise = (noise + noise.T) * 0.5
    index = jnp.arange(order)
    return jnp.where(index[:, None] == index[None, :], diagonal[:, None], noise)


def root_draw(key, order, salt):
    first, second = jax.random.split(jax.random.fold_in(key, 2000 + salt))
    diagonal = jax.random.uniform(first, (order,), jnp.float32, 0.5, 2.0)
    noise = jax.random.uniform(second, (order, order), jnp.float32, -1.0, 1.0) * (0.8 / math.sqrt(order))
    index = jnp.arange(order)
    return jnp.where(index[:, None] == index[None, :], diagonal[:, None], noise)


def draw_vectors(key, part):
    first, second = jax.random.split(jax.random.fold_in(key, 5))
    total = 8 * D + FF
    index = jnp.arange(total)
    gain_mask = (index < D) | (index >= 5 * D) & (index < 6 * D)
    gains = jax.random.uniform(first, (total,), jnp.float32, 0.6, 1.4)
    biases = jax.random.uniform(second, (total,), jnp.float32, -0.4, 0.4)
    return jnp.where(gain_mask, gains, biases)


def draw_qkv_left(key, part):
    return statistic(key, D, 1)


def draw_qkv_right(key, part):
    return statistic(key, 3 * D, 2)


def draw_qkv_left_root(key, part):
    return root_draw(key, D, 3)


def draw_qkv_right_root(key, part):
    return root_draw(key, 3 * D, 4)


def draw_out_left(key, part):
    return statistic(key, D, 5)


def draw_out_right(key, part):
    return statistic(key, D, 6)


def draw_out_left_root(key, part):
    return root_draw(key, D, 7)


def draw_out_right_root(key, part):
    return root_draw(key, D, 8)


def draw_fc_left(key, part):
    return statistic(key, D, 9)


def draw_fc_right(key, part):
    return statistic(key, FF, 10)


def draw_fc_left_root(key, part):
    return root_draw(key, D, 11)


def draw_fc_right_root(key, part):
    return root_draw(key, FF, 12)


def draw_proj_left(key, part):
    return statistic(key, FF, 13)


def draw_proj_right(key, part):
    return statistic(key, D, 14)


def draw_proj_left_root(key, part):
    return root_draw(key, FF, 15)


def draw_proj_right_root(key, part):
    return root_draw(key, D, 16)


def block_scale(rng, shape, cuts, least, largest):
    def one(dim, blocks):
        steps = jax.random.uniform(jax.random.fold_in(jax.random.fold_in(rng, 6), dim), (blocks,), jnp.float32, least / len(cuts), largest / len(cuts))
        return jnp.repeat(jnp.exp(steps), shape[dim] // blocks).reshape((-1,) + (1,) * (len(shape) - dim - 1))

    factor_of = one(*cuts[0])
    for cut in cuts[1:]:
        factor_of = factor_of * one(*cut)
    return factor_of


def profile(number_of, total, reach, lean):
    loads = [(1 << 20) // math.isqrt(rank ** lean) + 1 for rank in range(2, number_of + 1)]
    spare, holding = total - reach - (number_of - 1), [1] * (number_of - 1)
    while spare > 0:
        candidates = [i for i in range(number_of - 1) if holding[i] < reach]
        mass, budget = sum([loads[i] for i in candidates]), spare
        for i in candidates:
            extra = min(reach - holding[i], max(1, budget * loads[i] // mass), spare)
            holding[i] = holding[i] + extra
            spare = spare - extra
    return np.array([reach] + holding)


def uneven(rng, count, total, bound, lean):
    if count == 2:
        one = jax.random.randint(rng, (), max(1, total - bound), min(bound, total - 1) + 1)
        return jnp.stack([one, total - one])
    sizes = jnp.asarray(profile(count, total, bound, lean), jnp.int32)
    couples = (count - 1) // 2
    source_of, taker = sizes[1:1 + 2 * couples:2], sizes[2:2 + 2 * couples:2]
    margin = jnp.minimum(source_of - 1, bound - taker)
    shifted = jax.random.randint(jax.random.fold_in(rng, 1), (couples,), 0, 1 << 20) % (margin + 1)
    sizes = sizes.at[1:1 + 2 * couples:2].set(source_of - shifted).at[2:2 + 2 * couples:2].set(taker + shifted)
    return sizes[jax.random.permutation(jax.random.fold_in(rng, 2), count)]


def scatter_about(own_key, dims, width, most, cuts=(), kind=jnp.bfloat16):
    drawn = jax.random.normal(own_key, dims, jnp.float32) * width
    if len(cuts) > 0:
        drawn = block_scale(own_key, dims, cuts, -0.22, 0.18) * drawn
    return jnp.clip(drawn, min=-most, max=most).astype(kind)


def setup_inputs(seed: int = 0) -> dict:
    arg_keys = jax.random.split(jax.random.key(seed), 30)
    return {
        "tokens": scatter_about(arg_keys[0], (TOKENS, D), 1.0, 6.0, ((0, 32),)),
        "segments": jax.vmap(lambda own: jnp.searchsorted(jnp.cumsum(uneven(own, 3, SEQ, SEQ // 2, 0)), jnp.arange(SEQ), side="right"))(jax.random.split(arg_keys[1], SEQS)).reshape((SEQS, SEQ)).astype(jnp.int32),
        "cotangent": scatter_about(arg_keys[2], (TOKENS, D), 1.0, 6.0, ((0, 32),)),
        "vectors": draw_vectors(jax.random.fold_in(arg_keys[29], 71), 0),
        "vector_moment": scatter_about(arg_keys[4], (VEC,), 0.3, 4.0, ((0, 4),), jnp.float32),
        "qkv_weight": scatter_about(arg_keys[5], (D, 3 * D), D ** -0.5, 0.1875, ((0, 4), (1, 8)), jnp.float32),
        "qkv_moment": scatter_about(arg_keys[6], (D, 3 * D), 0.2, 3.0, ((0, 4), (1, 8)), jnp.float32),
        "qkv_left": draw_qkv_left(jax.random.fold_in(arg_keys[29], 71), 0),
        "qkv_right": draw_qkv_right(jax.random.fold_in(arg_keys[29], 71), 0),
        "qkv_left_root": draw_qkv_left_root(jax.random.fold_in(arg_keys[29], 71), 0),
        "qkv_right_root": draw_qkv_right_root(jax.random.fold_in(arg_keys[29], 71), 0),
        "out_weight": scatter_about(arg_keys[11], (D, D), (D // 8) ** -0.5, 0.5, ((0, 4), (1, 8)), jnp.float32),
        "out_moment": scatter_about(arg_keys[12], (D, D), 0.2, 3.0, ((0, 4), (1, 8)), jnp.float32),
        "out_left": draw_out_left(jax.random.fold_in(arg_keys[29], 71), 0),
        "out_right": draw_out_right(jax.random.fold_in(arg_keys[29], 71), 0),
        "out_left_root": draw_out_left_root(jax.random.fold_in(arg_keys[29], 71), 0),
        "out_right_root": draw_out_right_root(jax.random.fold_in(arg_keys[29], 71), 0),
        "fc_weight": scatter_about(arg_keys[17], (D, FF), D ** -0.5, 0.1875, ((0, 4), (1, 8)), jnp.float32),
        "fc_moment": scatter_about(arg_keys[18], (D, FF), 0.2, 3.0, ((0, 4), (1, 8)), jnp.float32),
        "fc_left": draw_fc_left(jax.random.fold_in(arg_keys[29], 71), 0),
        "fc_right": draw_fc_right(jax.random.fold_in(arg_keys[29], 71), 0),
        "fc_left_root": draw_fc_left_root(jax.random.fold_in(arg_keys[29], 71), 0),
        "fc_right_root": draw_fc_right_root(jax.random.fold_in(arg_keys[29], 71), 0),
        "proj_weight": scatter_about(arg_keys[23], (FF, D), FF ** -0.5, 0.09375, ((0, 4), (1, 8)), jnp.float32),
        "proj_moment": scatter_about(arg_keys[24], (FF, D), 0.2, 3.0, ((0, 4), (1, 8)), jnp.float32),
        "proj_left": draw_proj_left(jax.random.fold_in(arg_keys[29], 71), 0),
        "proj_right": draw_proj_right(jax.random.fold_in(arg_keys[29], 71), 0),
        "proj_left_root": draw_proj_left_root(jax.random.fold_in(arg_keys[29], 71), 0),
        "proj_right_root": draw_proj_right_root(jax.random.fold_in(arg_keys[29], 71), 0),
    }


EPSILON = 1e-05
DECAY = 0.5
MOMENTUM = 0.5
RATE = 0.03
PRECISE = lax.Precision.HIGHEST
MASKED = -1e+30

@jax.custom_vjp
def low(v):
    return lax.optimization_barrier(v.astype(jnp.bfloat16)).astype(jnp.float32)

@jax.custom_vjp
def low_back(v):
    return v

def low_keep(v):
    return (low(v), None)

def low_pass(kept, grad):
    return (grad,)

def back_keep(v):
    return (v, None)

def back_low(kept, grad):
    return (low(grad),)
low.defvjp(low_keep, low_pass)
low_back.defvjp(back_keep, back_low)

def norm_forward(values, gain, offset):
    centred = values - lax.optimization_barrier(jnp.mean(values, axis=-1, keepdims=True))
    scaled = centred * lax.rsqrt(lax.optimization_barrier(jnp.mean(centred * centred, axis=-1, keepdims=True)) + EPSILON)
    return scaled * gain + offset

def matmul(left, right):
    return jnp.dot(left, right, precision=PRECISE, preferred_element_type=jnp.float32)

def group_forward(rounded, inputs, labels):
    qkv_used, out_used, fc_used, proj_used, params = rounded
    seq_count = inputs.shape[0]
    flat_rows = inputs.reshape(seq_count * SEQ, D)
    gain_one = params[0:D]
    shift_one = params[D:2 * D]
    bias_query = params[2 * D:3 * D]
    bias_value = params[3 * D:4 * D]
    bias_out = params[4 * D:5 * D]
    gain_two = params[5 * D:6 * D]
    shift_two = params[6 * D:7 * D]
    bias_fc = params[7 * D:7 * D + FF]
    bias_proj = params[7 * D + FF:8 * D + FF]
    normed_one = low(norm_forward(flat_rows, gain_one, shift_one))
    qkv_bias = jnp.concatenate([bias_query, jnp.zeros_like(bias_query), bias_value])
    projected = low(low_back(matmul(normed_one, qkv_used) + qkv_bias))
    head_parts = projected.reshape(seq_count, SEQ, 3, HEADS, HEAD_DIM)
    queries = head_parts[:, :, 0]
    key_rows = head_parts[:, :, 1]
    value_rows = head_parts[:, :, 2]
    score_scale = HEAD_DIM ** (-0.5)
    scores = low_back(jnp.einsum('bqhd,bkhd->bhqk', queries, key_rows, precision=PRECISE) * score_scale)
    position = jnp.arange(SEQ)
    allowed = (labels[:, :, None] == labels[:, None, :]) & (position[:, None] >= position[None, :])
    attention = jax.nn.softmax(jnp.where(allowed[:, None], scores, MASKED), axis=-1)
    attended = jnp.einsum('bhqk,bkhd->bqhd', low(attention), value_rows, precision=PRECISE)
    attended = low(low_back(attended.reshape(seq_count * SEQ, D)))
    branch = low_back(matmul(attended, out_used) + bias_out)
    middle = flat_rows + branch
    normed_two = low(norm_forward(middle, gain_two, shift_two))
    pre_act = low_back(matmul(normed_two, fc_used) + bias_fc)
    activated = low(jax.nn.gelu(pre_act, approximate=True))
    mlp_out = low_back(matmul(activated, proj_used) + bias_proj)
    return (middle + mlp_out).reshape(seq_count, SEQ, D)

def layer_forward(params, inputs, labels):
    rounded = tuple((low(member) for member in params))
    per_group = min(SEQS, max(1, 4096 // SEQ))
    group_total = SEQS // per_group
    shaped = inputs.reshape(group_total, per_group, SEQ, D)
    label_groups = labels.reshape(group_total, per_group, SEQ)

    def one_group(pieces):
        return group_forward(rounded, pieces[0], pieces[1])
    results = lax.map(jax.checkpoint(one_group), (shaped, label_groups))
    return results.reshape(SEQS, SEQ, D)

def shampoo(weight, moment, left, right, left_root, right_root, gradient):
    row_count = gradient.shape[0]
    col_count = gradient.shape[1]
    new_left = DECAY * left + (1.0 - DECAY) / col_count * matmul(gradient, gradient.T)
    new_right = DECAY * right + (1.0 - DECAY) / row_count * matmul(gradient.T, gradient)
    direction = matmul(left_root, matmul(gradient, right_root))
    new_moment = MOMENTUM * moment + direction
    new_weight = weight - RATE * new_moment
    return (gradient, new_left, new_right, new_moment, new_weight, new_weight.astype(jnp.bfloat16))

def reference(tokens, segments, cotangent, vectors, vector_moment, qkv_weight, qkv_moment, qkv_left, qkv_right, qkv_left_root, qkv_right_root, out_weight, out_moment, out_left, out_right, out_left_root, out_right_root, fc_weight, fc_moment, fc_left, fc_right, fc_left_root, fc_right_root, proj_weight, proj_moment, proj_left, proj_right, proj_left_root, proj_right_root):
    inputs = tokens.astype(jnp.float32).reshape(SEQS, SEQ, D)
    forward = functools.partial(layer_forward, labels=segments.reshape(SEQS, SEQ))
    params = (qkv_weight, out_weight, fc_weight, proj_weight, vectors)
    result, pullback = jax.vjp(forward, params, inputs)
    param_grads, input_grads = pullback(cotangent.astype(jnp.float32).reshape(SEQS, SEQ, D))
    factor = 1.0 / math.sqrt(TOKENS)
    grads = [member * factor for member in param_grads]
    qkv_new = shampoo(qkv_weight, qkv_moment, qkv_left, qkv_right, qkv_left_root, qkv_right_root, grads[0])
    out_new = shampoo(out_weight, out_moment, out_left, out_right, out_left_root, out_right_root, grads[1])
    fc_new = shampoo(fc_weight, fc_moment, fc_left, fc_right, fc_left_root, fc_right_root, grads[2])
    proj_new = shampoo(proj_weight, proj_moment, proj_left, proj_right, proj_left_root, proj_right_root, grads[3])
    vector_grad = grads[4]
    new_vector_moment = MOMENTUM * vector_moment + vector_grad
    new_vectors = vectors - RATE * new_vector_moment
    return (result.reshape(TOKENS, D).astype(jnp.bfloat16), input_grads.reshape(TOKENS, D).astype(jnp.bfloat16), qkv_new[0], qkv_new[1], qkv_new[2], qkv_new[3], qkv_new[4], qkv_new[5], out_new[0], out_new[1], out_new[2], out_new[3], out_new[4], out_new[5], fc_new[0], fc_new[1], fc_new[2], fc_new[3], fc_new[4], fc_new[5], proj_new[0], proj_new[1], proj_new[2], proj_new[3], proj_new[4], proj_new[5], vector_grad, new_vector_moment, new_vectors)
```

```python
import math

import jax
import jax.numpy as jnp
import numpy as np
from jax import lax
from jax.experimental import pallas as pl
from jax.experimental.pallas import tpu as pltpu
from jax.sharding import Mesh
from jax.sharding import PartitionSpec as P

HEADS = 16
HEAD_DIM = 64
EPSILON = 1e-05
DECAY = 0.5
MOMENTUM = 0.5
RATE = 0.03
MASKED = -1e30
ROOT_TWO_PI = math.sqrt(2.0 / math.pi)
BF16 = jnp.bfloat16
F32 = jnp.float32
PLANE = ("y", "x")
CHIPS = ("y", "x", "in")
ALL = ("y", "x", "c", "in")


def dot(left, right):
    return jnp.dot(left, right, preferred_element_type=F32)


def dot_tn(left, right):
    return lax.dot_general(left, right, (((0,), (0,)), ((), ())), preferred_element_type=F32)


def dot_nt(left, right):
    return lax.dot_general(left, right, (((1,), (1,)), ((), ())), preferred_element_type=F32)


def lane_half(shape, half):
    return (lax.broadcasted_iota(jnp.int32, shape, 1) // HEAD_DIM) == half


def softmax_rows(scores):
    shifted = jnp.exp(scores - jnp.max(scores, axis=-1, keepdims=True))
    return shifted / jnp.sum(shifted, axis=-1, keepdims=True)


def attention_forward(qkv, bias):
    sequences, length, _ = bias.shape
    width = qkv.shape[1] // 3
    pair = 2 * HEAD_DIM
    scale = HEAD_DIM ** (-0.5)

    def body(qkv_ref, bias_ref, out_ref):
        for seq in range(sequences):
            rows = slice(seq * length, (seq + 1) * length)
            mask = bias_ref[seq]
            for col in range(0, width, pair):
                queries = qkv_ref[rows, col : col + pair]
                key_rows = qkv_ref[rows, width + col : width + col + pair]
                value_rows = qkv_ref[rows, 2 * width + col : 2 * width + col + pair]
                parts = []
                for half in range(2):
                    own = jnp.where(lane_half(queries.shape, half), queries, jnp.zeros_like(queries))
                    probs = softmax_rows(dot_nt(own, key_rows) * scale + mask)
                    parts.append(dot(probs.astype(BF16), value_rows))
                picked = jnp.where(lane_half(parts[0].shape, 0), parts[0], parts[1])
                out_ref[rows, col : col + pair] = picked.astype(BF16)

    return pl.pallas_call(
        body,
        out_shape=jax.ShapeDtypeStruct((qkv.shape[0], width), BF16),
        in_specs=[pl.BlockSpec(memory_space=pltpu.VMEM)] * 2,
        out_specs=pl.BlockSpec(memory_space=pltpu.VMEM),
        name="attention_forward",
    )(qkv, bias)


def attention_backward(qkv, bias, grad):
    sequences, length, _ = bias.shape
    width = qkv.shape[1] // 3
    pair = 2 * HEAD_DIM
    scale = HEAD_DIM ** (-0.5)

    def body(qkv_ref, bias_ref, grad_ref, out_ref):
        for seq in range(sequences):
            rows = slice(seq * length, (seq + 1) * length)
            mask = bias_ref[seq]
            for col in range(0, width, pair):
                queries = qkv_ref[rows, col : col + pair]
                key_rows = qkv_ref[rows, width + col : width + col + pair]
                value_rows = qkv_ref[rows, 2 * width + col : 2 * width + col + pair]
                grads = grad_ref[rows, col : col + pair]
                found = []
                for half in range(2):
                    lanes = lane_half(queries.shape, half)
                    own = jnp.where(lanes, queries, jnp.zeros_like(queries))
                    probs = softmax_rows(dot_nt(own, key_rows) * scale + mask)
                    own_grad = jnp.where(lanes, grads, jnp.zeros_like(grads))
                    grad_probs = dot_nt(own_grad, value_rows)
                    row_dot = jnp.sum(probs * grad_probs, axis=-1, keepdims=True)
                    grad_scores = (probs * (grad_probs - row_dot)).astype(BF16)
                    found.append(
                        (
                            dot(grad_scores, key_rows) * scale,
                            dot_tn(grad_scores, queries) * scale,
                            dot_tn(probs.astype(BF16), grads),
                        )
                    )
                low_lanes = lane_half((length, pair), 0)
                for third in range(3):
                    picked = jnp.where(low_lanes, found[0][third], found[1][third])
                    start = third * width + col
                    out_ref[rows, start : start + pair] = picked.astype(BF16)

    return pl.pallas_call(
        body,
        out_shape=jax.ShapeDtypeStruct(qkv.shape, BF16),
        in_specs=[pl.BlockSpec(memory_space=pltpu.VMEM)] * 3,
        out_specs=pl.BlockSpec(memory_space=pltpu.VMEM),
        name="attention_backward",
    )(qkv, bias, grad)


def assemble(pieces, places, axis):
    count, shape = len(pieces), pieces[0].shape
    size = shape[axis]

    def body(place_ref, *refs):
        for k in range(count):
            span = pl.ds(pl.multiple_of(place_ref[k] * size, size), size)
            if axis == 0:
                refs[count][span, :] = refs[k][...]
            else:
                refs[count][:, span] = refs[k][...]

    in_vmem = pl.BlockSpec(memory_space=pltpu.VMEM)
    whole = tuple(extent * (count if n == axis else 1) for n, extent in enumerate(shape))
    return pl.pallas_call(
        body,
        out_shape=jax.ShapeDtypeStruct(whole, pieces[0].dtype),
        in_specs=[pl.BlockSpec(memory_space=pltpu.SMEM)] + [in_vmem] * count,
        out_specs=in_vmem,
        name="assemble",
    )(jnp.stack(places).astype(jnp.int32), *pieces)


def whole(array):
    return pl.BlockSpec(array.shape, lambda step: (0,) * len(array.shape))


def column_kernel(own, blocks, which, right_root, numbers):
    width, cols = own.shape
    count, _, rows, share = blocks.shape
    chunks = width // rows

    def body(number_ref, own_ref, block_ref, right_ref, mine_ref, theirs_ref, left_ref):
        core, depth = number_ref[0], number_ref[1]
        near = own_ref[pl.ds(pl.multiple_of(depth * rows, rows), rows), :]

        @pl.loop(0, chunks)
        def _(d):
            chunk = number_ref[2 + d]
            for g in range(count // chunks):
                left_ref[:, g * share : (g + 1) * share] = block_ref[g * chunks + chunk, 0]
            image = dot(left_ref[...], own_ref[...]).astype(BF16)
            span = pl.ds(pl.multiple_of(d * rows, rows), rows)
            for pick, target in ((core, mine_ref), (1 - core, theirs_ref)):
                right = right_ref[:, pl.ds(pl.multiple_of(pick * cols, cols), cols)].astype(BF16)
                start = pl.multiple_of(chunk * rows + pick * share, share)
                target[span, :cols] = dot(image, right).astype(target.dtype)
                left = dot_nt(near, own_ref[pl.ds(start, share), :])
                target[span, cols:] = left.astype(target.dtype)

    shape = (width, cols + share)
    return pl.pallas_call(
        body,
        grid=(1,),
        out_shape=(jax.ShapeDtypeStruct(shape, F32), jax.ShapeDtypeStruct(shape, BF16)),
        in_specs=[
            pl.BlockSpec(memory_space=pltpu.SMEM),
            whole(own),
            pl.BlockSpec((count, 1, rows, share), lambda step: (0, which, 0, 0)),
            whole(right_root),
        ],
        out_specs=(pl.BlockSpec(shape, lambda step: (0, 0)),) * 2,
        scratch_shapes=[pltpu.VMEM((rows, width), BF16)],
        compiler_params=pltpu.CompilerParams(vmem_limit_bytes=40 << 20),
        name="column_terms",
    )(numbers, own, blocks, right_root)


def row_kernel(own, blocks, which, left_root, numbers):
    count, width = own.shape
    devices, _, rows, share = blocks.shape
    chunks = width // rows
    tall = left_root.shape[0]
    piece = tall + 2 * share

    def body(number_ref, own_ref, block_ref, left_ref, mine_ref, theirs_ref, right_ref):
        core, depth = number_ref[0], number_ref[1]
        targets = ((core, mine_ref), (1 - core, theirs_ref))
        near = own_ref[:, pl.ds(pl.multiple_of(depth * rows, rows), rows)]
        for d in range(chunks):
            chunk = number_ref[2 + d]
            for k, (pick, target) in enumerate(targets):
                part = pl.ds(pl.multiple_of(pick * share, share), share)
                lanes = slice((k * chunks + d) * share, (k * chunks + d + 1) * share)
                for g in range(devices // chunks):
                    right_ref[g * share : (g + 1) * share, lanes] = block_ref[
                        g * chunks + chunk, 0, part, :
                    ]
                start = pl.multiple_of(chunk * rows + pick * share, share)
                right = dot_tn(own_ref[:, pl.ds(start, share)], near).astype(target.dtype)
                low = d * piece + tall
                target[low : low + share, :] = right[:, :share]
                target[low + share : low + 2 * share, :] = right[:, share:]
        image = dot(own_ref[...], right_ref[...]).astype(BF16)
        for first in range(0, tall, rows):
            ahead = dot(left_ref[first : first + rows, :].astype(BF16), image)
            for k, (_, target) in enumerate(targets):
                for d in range(chunks):
                    lanes = slice((k * chunks + d) * share, (k * chunks + d + 1) * share)
                    low = d * piece + first
                    target[low : low + rows, :] = ahead[:, lanes].astype(target.dtype)

    shape = (chunks * piece, share)
    return pl.pallas_call(
        body,
        grid=(1,),
        out_shape=(jax.ShapeDtypeStruct(shape, F32), jax.ShapeDtypeStruct(shape, BF16)),
        in_specs=[
            pl.BlockSpec(memory_space=pltpu.SMEM),
            whole(own),
            pl.BlockSpec((devices, 1, rows, share), lambda step: (0, which, 0, 0)),
            whole(left_root),
        ],
        out_specs=(pl.BlockSpec(shape, lambda step: (0, 0)),) * 2,
        scratch_shapes=[pltpu.VMEM((width, width), BF16)],
        compiler_params=pltpu.CompilerParams(vmem_limit_bytes=40 << 20),
        name="row_terms",
    )(numbers, own, blocks, left_root)


class Place:
    def __init__(self):
        self.rows = lax.axis_size("y")
        self.plane = self.rows * lax.axis_size("x")
        self.depth = lax.axis_size("in")
        self.q = lax.axis_index("y") * lax.axis_size("x") + lax.axis_index("x")
        self.c = lax.axis_index("c")
        self.z = lax.axis_index("in")
        self.last = {}

    def send(self, value, axes, pairs, lane=None):
        if lane in self.last:
            value, _ = lax.optimization_barrier((value, self.last[lane]))
        value = lax.ppermute(value, axes, pairs)
        if lane is not None:
            self.last[lane] = value
        return value

    def swap_core(self, value):
        return self.send(value, "c", [(0, 1), (1, 0)])

    def swap_plane(self, value, distance):
        pairs = [(k, k ^ distance) for k in range(self.plane)]
        return self.send(value, PLANE, pairs, distance)

    def ring(self, value):
        return self.send(value, "in", [(k, (k + 1) % self.depth) for k in range(self.depth)], "z")

    def on_chips(self, value, target, lane):
        pairs = []
        for q in range(self.plane):
            for z in range(self.depth):
                found = target(q, z)
                if found is not None:
                    pairs.append((q * self.depth + z, found[0] * self.depth + found[1]))
        return self.send(value, CHIPS, pairs, lane)

    def by_core(self, own, other):
        return jnp.where(self.c == 0, own, other), jnp.where(self.c == 0, other, own)

    def mine(self, pair):
        return jnp.where(self.c == 0, pair[0], pair[1])

    def theirs(self, pair):
        return jnp.where(self.c == 0, pair[1], pair[0])

    def shuffle(self, values, index):
        values = list(values)
        bit = 1
        while bit < len(values):
            on = (index // bit) % 2 == 1
            values = [jnp.where(on, values[k ^ bit], values[k]) for k in range(len(values))]
            bit *= 2
        return values

    def ring_pieces(self, value):
        pieces = [value]
        for _ in range(self.depth - 1):
            pieces.append(self.ring(pieces[-1]))
        return pieces

    def gather_depth(self, value, axis=0):
        places = [(self.z - k) % self.depth for k in range(self.depth)]
        return assemble(self.ring_pieces(value), places, axis)

    def transpose_chips(self, value):
        return self.on_chips(value, lambda q, z: (z, q), "z")

    def spread_plane(self, value):
        q, z = self.q, self.z
        if self.plane != 4:
            total = jnp.where(q == z, value, jnp.zeros_like(value))
            for d in range(1, self.plane):
                total = total + self.on_chips(
                    value, lambda a, b, d=d: (a ^ d, b) if a == b else None, d
                )
            return total
        half = value.shape[0] // 2
        low, high = value[:half], value[half:]
        low_x = self.on_chips(low, lambda a, b: (a ^ 1, b) if a == b else None, 1)
        high_y = self.on_chips(high, lambda a, b: (a ^ 2, b) if a == b else None, 2)
        high_x = self.on_chips(
            jnp.where(q == z, high, high_y), lambda a, b: (a ^ 1, b) if a ^ b in (0, 2) else None, 1
        )
        low_y = self.on_chips(
            jnp.where(q == z, low, low_x), lambda a, b: (a ^ 2, b) if a ^ b in (0, 1) else None, 2
        )
        apart = q ^ z
        low = jnp.where(apart == 0, low, jnp.where(apart == 1, low_x, low_y))
        high = jnp.where(apart == 0, high, jnp.where(apart == 2, high_y, high_x))
        return jnp.concatenate([low, high])

    def gather_tokens(self, value):
        mine = jnp.concatenate(self.gather_plane(value))
        return jnp.concatenate([mine, self.swap_core(mine)])

    def reduce_tokens(self, mine, theirs):
        total = mine + self.swap_core(theirs.astype(BF16)).astype(F32)
        return self.reduce_plane(jnp.split(total, self.plane))

    def gather_plane(self, value):
        if self.plane != 4:
            return [value] + [self.swap_plane(value, d) for d in range(1, self.plane)]
        half = value.shape[0] // 2
        by_x = self.swap_plane(value, 1)
        by_y = self.swap_plane(value, 2)
        first = self.swap_plane(by_y[:half], 1)
        second = self.swap_plane(by_x[half:], 2)
        return [value, by_x, by_y, jnp.concatenate([first, second])]

    def reduce_plane(self, values):
        if self.plane != 4:
            total = values[0]
            for d in range(1, self.plane):
                total = total + self.swap_plane(values[d].astype(BF16), d).astype(F32)
            return total
        half = values[0].shape[0] // 2
        far = values[3].astype(BF16)
        first = self.swap_plane(far[:half], 1)
        second = self.swap_plane(far[half:], 2)
        to_y = jnp.concatenate([values[2][:half] + first.astype(F32), values[2][half:]]).astype(BF16)
        to_x = jnp.concatenate([values[1][:half], values[1][half:] + second.astype(F32)]).astype(BF16)
        by_x = self.swap_plane(to_x, 1)
        by_y = self.swap_plane(to_y, 2)
        return values[0] + by_x.astype(F32) + by_y.astype(F32)

    def reduce_depth(self, value, sent=BF16, axis=0):
        size = value.shape[axis] // self.depth
        total = None
        for step in range(self.depth):
            place = (self.z - 1 - step) % self.depth
            chunk = lax.dynamic_slice_in_dim(value, place * size, size, axis)
            total = chunk if total is None else total.astype(F32) + chunk
            if step < self.depth - 1:
                total = self.ring(total.astype(sent))
        return total


def norm_parts(values):
    centred = values - jnp.mean(values, axis=-1, keepdims=True)
    spread = lax.rsqrt(jnp.mean(centred * centred, axis=-1, keepdims=True) + EPSILON)
    return centred * spread, spread


def norm_backward(grad, scaled, spread, gain):
    inner = grad * gain
    mean_one = jnp.mean(inner, axis=-1, keepdims=True)
    mean_two = jnp.mean(inner * scaled, axis=-1, keepdims=True)
    return spread * (inner - mean_one - scaled * mean_two)


def gelu(values):
    return 0.5 * values * (1.0 + jnp.tanh(ROOT_TWO_PI * (values + 0.044715 * values**3)))


def gelu_slope(values):
    squared = values * values
    bent = jnp.tanh(ROOT_TWO_PI * (values + 0.044715 * squared * values))
    return 0.5 * (1.0 + bent) + 0.5 * values * (1.0 - bent * bent) * (
        ROOT_TWO_PI * (1.0 + 3.0 * 0.044715 * squared)
    )


def on_device(
    tokens,
    segments,
    cotangent,
    vectors,
    vector_moment,
    qkv_weight,
    qkv_moment,
    qkv_left,
    qkv_right,
    qkv_left_root,
    qkv_right_root,
    out_weight,
    out_moment,
    out_left,
    out_right,
    out_left_root,
    out_right_root,
    fc_weight,
    fc_moment,
    fc_left,
    fc_right,
    fc_left_root,
    fc_right_root,
    proj_weight,
    proj_moment,
    proj_left,
    proj_right,
    proj_left_root,
    proj_right_root,
):
    here = Place()
    plane, depth = here.plane, here.depth
    length, width = tokens.shape
    z, q, c = here.z, here.q, here.c

    def pair_columns(share):
        return jnp.concatenate(here.by_core(share, here.swap_core(share)), axis=1)

    def by_parity(pair):
        rows, cols = pair.shape
        split = pair.reshape(rows, cols // (2 * HEAD_DIM), 2, HEAD_DIM)
        return here.mine((split[:, :, 0], split[:, :, 1])).reshape(rows, cols // 2)

    qkv_share = by_parity(pair_columns(qkv_weight.astype(BF16)))
    fc_share = fc_weight.astype(BF16)
    proj_split = proj_weight.astype(BF16).reshape(2, -1, proj_weight.shape[1])
    proj_share = jnp.concatenate(
        here.by_core(here.mine(proj_split), here.swap_core(here.theirs(proj_split))), axis=1
    )
    out_split = out_weight.astype(BF16).reshape(-1, 2, HEAD_DIM, out_weight.shape[1])
    out_split = (
        out_split[:, 0].reshape(-1, out_weight.shape[1]),
        out_split[:, 1].reshape(-1, out_weight.shape[1]),
    )
    out_share = jnp.concatenate(
        here.by_core(here.mine(out_split), here.swap_core(here.theirs(out_split))), axis=1
    )

    plane_cotangent = here.gather_tokens(cotangent)
    qkv_parts = here.gather_plane(here.gather_depth(qkv_share))
    vector_whole = jnp.roll(
        jnp.concatenate(here.ring_pieces(vectors.astype(BF16))[::-1]), (z + 1) * vectors.shape[0]
    )
    out_parts = here.gather_plane(here.gather_depth(out_share))
    out_full = jnp.concatenate(here.shuffle(out_parts, q), axis=1)
    fc_full = here.gather_depth(fc_share)
    proj_full = here.gather_depth(here.transpose_chips(proj_share), axis=1)

    share_rows, share_cols = qkv_left_root.shape
    right_root = proj_right_root.astype(BF16)
    root_blocks = lax.all_gather(
        jnp.stack(
            [root.astype(BF16) for root in (qkv_left_root, out_left_root, fc_left_root)]
            + [jnp.concatenate([right_root[:, :share_cols], right_root[:, share_cols:]])]
        ),
        ALL,
    )
    numbers = jnp.stack([c, z] + [q ^ d for d in range(plane)]).astype(jnp.int32)

    params = vector_whole.astype(F32)
    unit = fc_weight.shape[1]
    hidden = unit * 2 * plane
    gain_one, shift_one, bias_query, bias_value, bias_out, gain_two, shift_two = (
        params[k * width : (k + 1) * width] for k in range(7)
    )
    bias_fc = lax.dynamic_slice_in_dim(params, 7 * width + (2 * q + c) * unit, unit)
    bias_proj = params[7 * width + hidden :]

    pair_tokens = jnp.concatenate([tokens, here.swap_core(tokens)])
    labels = jnp.concatenate([segments, here.swap_core(segments)])
    position = jnp.arange(length)
    allowed = (labels[:, :, None] == labels[:, None, :]) & (position[:, None] >= position[None, :])
    mask = jnp.where(allowed, 0.0, MASKED).astype(F32)

    inputs = pair_tokens.astype(F32)
    scaled_one, spread_one = norm_parts(inputs)
    normed_one = (scaled_one * gain_one + shift_one).astype(BF16)
    qkv_bias = jnp.concatenate([bias_query, jnp.zeros_like(bias_query), bias_value])
    qkv_bias = qkv_bias.reshape(-1, 2, HEAD_DIM)
    qkv_bias = here.mine((qkv_bias[:, 0], qkv_bias[:, 1])).reshape(-1)
    projected = jnp.concatenate(
        here.shuffle([dot(normed_one, part) for part in qkv_parts], q), axis=1
    )
    projected = (projected + qkv_bias).astype(BF16)
    attended = attention_forward(projected, mask)
    branch = dot(attended[:length], out_full) + here.swap_core(dot(attended[length:], out_full))
    middle = inputs[:length] + (branch + bias_out)
    scaled_two, spread_two = norm_parts(middle)
    normed_two = here.gather_tokens((scaled_two * gain_two + shift_two).astype(BF16))
    pre_act = dot(normed_two, fc_full) + bias_fc
    activated = gelu(pre_act).astype(BF16)

    token_total = length * 2 * plane * depth
    factor = 1.0 / math.sqrt(token_total)
    half = plane * length
    proj_sum = here.reduce_depth(dot_tn(activated, plane_cotangent), axis=1)
    grad_pre = (dot_nt(plane_cotangent, proj_full) * gelu_slope(pre_act)).astype(BF16)
    grad_normed_two = here.reduce_tokens(
        dot_nt(grad_pre[:half], fc_full), dot_nt(grad_pre[half:], fc_full)
    )
    fc_grad = here.reduce_depth(dot_tn(normed_two, grad_pre)) * factor
    output = here.reduce_tokens(
        dot(activated[:half], proj_full), dot(activated[half:], proj_full)
    )
    output = (middle + (output + bias_proj)).astype(BF16)

    proj_scaled = (proj_sum * factor).astype(BF16)
    proj_rows = here.transpose_chips(proj_scaled)
    proj_own = here.gather_depth(proj_scaled, axis=1)
    fc_own = here.gather_depth(fc_grad.astype(BF16))
    far_rows = jnp.concatenate(here.shuffle(here.gather_plane(proj_rows), q), axis=1)
    far_rows = jnp.concatenate(here.by_core(far_rows, here.swap_core(far_rows)))

    grad_top = cotangent.astype(F32)
    grad_middle = grad_top + norm_backward(grad_normed_two, scaled_two, spread_two, gain_two)
    own_branch = grad_middle.astype(BF16)
    grad_branch = jnp.concatenate([own_branch, here.swap_core(own_branch)])
    grad_attended = dot_nt(grad_branch, out_full).astype(BF16)
    grad_heads = attention_backward(projected, mask, grad_attended)
    head_blocks = here.shuffle(jnp.split(grad_heads, plane, axis=1), q)
    branch_blocks = here.shuffle(jnp.split(grad_branch, plane, axis=1), q)

    rows_own, qkv_cols = qkv_weight.shape
    out_cols = out_weight.shape[1]

    def out_term(block):
        term = dot_tn(attended, block).reshape(depth, -1, 2 * out_cols)
        term = jnp.concatenate([term[:, :, :out_cols], term[:, :, out_cols:]], axis=1)
        return term.reshape(width, out_cols)

    first_sum = here.reduce_depth(
        here.reduce_plane(
            [
                jnp.concatenate([dot_tn(normed_one, head), out_term(branch)], axis=1)
                for head, branch in zip(head_blocks, branch_blocks)
            ]
        )
    )
    first_sum = first_sum * factor

    other_one = sum(dot_nt(block[length:], part) for block, part in zip(head_blocks, qkv_parts))
    grad_normed_one = sum(dot_nt(block[:length], part) for block, part in zip(head_blocks, qkv_parts))
    grad_normed_one = grad_normed_one + here.swap_core(other_one)
    own_scaled = scaled_one[:length]
    grad_in = norm_backward(grad_normed_one, own_scaled, spread_one[:length], gain_one)
    input_grad = (grad_middle + grad_in).astype(BF16)

    proj_halves = jnp.split(proj_rows, 2, axis=1)
    proj_grad = jnp.concatenate(
        here.by_core(here.mine(proj_halves), here.swap_core(here.theirs(proj_halves)))
    ).astype(F32)

    qkv_parity = first_sum[:, :qkv_cols].reshape(rows_own, -1, 1, HEAD_DIM)
    qkv_pair = jnp.concatenate(here.by_core(qkv_parity, here.swap_core(qkv_parity)), axis=2)
    qkv_pair = qkv_pair.reshape(rows_own, 2 * qkv_cols)
    qkv_grad = here.mine((qkv_pair[:, :qkv_cols], qkv_pair[:, qkv_cols:]))
    out_halves = jnp.split(first_sum[:, qkv_cols:], 2)
    out_pair = here.by_core(here.mine(out_halves), here.swap_core(here.theirs(out_halves)))
    out_grad = jnp.stack(
        [part.reshape(-1, HEAD_DIM, out_cols) for part in out_pair], axis=1
    ).reshape(out_weight.shape)

    def sum_over_group(mine, theirs):
        total = mine + here.swap_core(theirs).astype(F32)
        return here.reduce_plane(jnp.split(total, plane))

    aligned = share_cols % 128 == 0

    def column_terms(own, which, right_root):
        if aligned:
            return column_kernel(own, root_blocks, which, right_root, numbers)
        blocks = root_blocks.reshape(2 * plane, depth, 4, share_rows, share_cols)[:, :, which]
        left_root = blocks.transpose(1, 2, 0, 3).reshape(depth, share_rows, width)
        left_root = jnp.concatenate(here.shuffle(list(left_root), q))
        image = dot(left_root, own).astype(BF16)
        right_halves = jnp.split(right_root.astype(BF16), 2, axis=1)
        left = dot_nt(lax.dynamic_slice_in_dim(own, z * rows_own, rows_own), own)
        left = here.shuffle(jnp.split(left, plane, axis=1), q)
        left = jnp.split(jnp.concatenate(left), 2, axis=1)
        mine, theirs = (
            jnp.concatenate([dot(image, pick(right_halves)), pick(left)], axis=1)
            for pick in (here.mine, here.theirs)
        )
        return mine, theirs.astype(BF16)

    def row_terms(own, which, left_root):
        if aligned:
            return row_kernel(own, root_blocks, which, left_root, numbers)
        blocks = root_blocks.reshape(2 * plane, depth, 4, 2, share_rows // 2, share_cols)[:, :, which]
        chunk = width // depth
        right = dot_tn(own, lax.dynamic_slice_in_dim(own, z * chunk, chunk, 1))
        right = here.shuffle(jnp.split(right, plane), q)
        left_root = left_root.astype(BF16)
        found = []
        for pick in (here.mine, here.theirs):
            root = pick((blocks[:, :, 0], blocks[:, :, 1]))
            root = [root[:, r].reshape(width, share_cols) for r in range(depth)]
            root = jnp.concatenate(here.shuffle(root, q), axis=1)
            ahead = jnp.split(dot(left_root, dot(own, root).astype(BF16)), plane, axis=1)
            stats = [
                jnp.concatenate(jnp.split(pick(jnp.split(pair, 2)), 2, axis=1)) for pair in right
            ]
            found.append(
                jnp.concatenate([jnp.concatenate(parts) for parts in zip(ahead, stats)])
            )
        return found[0], found[1].astype(BF16)

    def far_columns(own):
        far = here.spread_plane(own)
        return here.by_core(far, here.swap_core(far))

    proj_total = sum_over_group(*row_terms(proj_own, 3, proj_left_root))
    proj_direction = proj_total[: proj_weight.shape[0]]
    proj_right_sum = jnp.concatenate(jnp.split(proj_total[proj_weight.shape[0] :], 2), axis=1)
    proj_left_sum = dot_nt(far_rows, proj_own)

    unit_cols = fc_weight.shape[1]
    fc_total = sum_over_group(*column_terms(fc_own, 2, fc_right_root))
    fc_direction = here.transpose_chips(fc_total[:, :unit_cols].astype(BF16)).astype(F32)
    fc_left_sum = fc_total[:, unit_cols:]

    first_own = here.gather_depth(jnp.concatenate([qkv_grad, out_grad], axis=1).astype(BF16))
    qkv_own, out_own = first_own[:, :qkv_cols], first_own[:, qkv_cols:]
    qkv_total = sum_over_group(*column_terms(qkv_own, 0, qkv_right_root))
    qkv_direction = here.transpose_chips(qkv_total[:, :qkv_cols].astype(BF16)).astype(F32)
    qkv_left_sum = qkv_total[:, qkv_cols:]
    out_total = sum_over_group(*column_terms(out_own, 1, out_right_root))
    out_direction = here.transpose_chips(out_total[:, :out_cols].astype(BF16)).astype(F32)
    out_left_sum = out_total[:, out_cols:]

    fc_right_sum = dot_tn(fc_own, jnp.concatenate(far_columns(fc_own), axis=1))
    first_far = far_columns(first_own)
    qkv_right_sum = dot_tn(
        qkv_own, jnp.concatenate([part[:, :qkv_cols] for part in first_far], axis=1)
    )
    out_right_sum = dot_tn(
        out_own, jnp.concatenate([part[:, qkv_cols:] for part in first_far], axis=1)
    )

    def interleave(value, block):
        value = value.reshape(-1, 1, block)
        zeros = jnp.zeros_like(value)
        return jnp.concatenate(here.by_core(value, zeros), axis=1).reshape(-1)

    head_sums = interleave(jnp.sum(grad_heads.astype(F32), axis=0), HEAD_DIM)
    fc_bias_terms = lax.dynamic_update_slice_in_dim(
        jnp.zeros((hidden,), F32), jnp.sum(grad_pre.astype(F32), axis=0), (2 * q + c) * unit, 0
    )
    vector_terms = jnp.concatenate(
        [
            jnp.sum(grad_normed_one * own_scaled, axis=0),
            jnp.sum(grad_normed_one, axis=0),
            head_sums[:width],
            head_sums[2 * width :],
            jnp.sum(own_branch.astype(F32), axis=0),
            jnp.sum(grad_normed_two * scaled_two, axis=0),
            jnp.sum(grad_normed_two, axis=0),
            fc_bias_terms,
            jnp.sum(grad_top, axis=0),
        ]
    )
    vector_sum = here.swap_core(vector_terms) + vector_terms
    vector_sum = here.reduce_depth(vector_sum.reshape(-1, 128), F32)
    distance = 1
    while distance < plane:
        vector_sum = vector_sum + here.swap_plane(vector_sum, distance)
        distance *= 2
    vector_grad = vector_sum.reshape(-1) * factor

    results = []
    for grad, weight, moment, left, right, found, row_total, col_total in (
        (
            qkv_grad,
            qkv_weight,
            qkv_moment,
            qkv_left,
            qkv_right,
            (qkv_left_sum, qkv_right_sum, qkv_direction),
            width,
            3 * width,
        ),
        (
            out_grad,
            out_weight,
            out_moment,
            out_left,
            out_right,
            (out_left_sum, out_right_sum, out_direction),
            width,
            width,
        ),
        (
            fc_grad,
            fc_weight,
            fc_moment,
            fc_left,
            fc_right,
            (fc_left_sum, fc_right_sum, fc_direction),
            width,
            hidden,
        ),
        (
            proj_grad,
            proj_weight,
            proj_moment,
            proj_left,
            proj_right,
            (proj_left_sum, proj_right_sum, proj_direction),
            hidden,
            width,
        ),
    ):
        left_sum, right_sum, direction = found
        new_moment = MOMENTUM * moment + direction
        new_weight = weight - RATE * new_moment
        results += [
            grad,
            DECAY * left + (1.0 - DECAY) / col_total * left_sum,
            DECAY * right + (1.0 - DECAY) / row_total * right_sum,
            new_moment,
            new_weight,
            new_weight.astype(BF16),
        ]
    new_vector_moment = MOMENTUM * vector_moment + vector_grad
    new_vectors = vectors - RATE * new_vector_moment
    return (output, input_grad, *results, vector_grad, new_vector_moment, new_vectors)


def solution(mesh):
    groups, depth = mesh.shape["grp"], mesh.shape["in"]
    fine = Mesh(mesh.devices.reshape(groups // 4, 2, 2, depth), ALL)
    grp = ("y", "x", "c")
    tokens, cols, rows, flat = P(ALL, None), P("in", grp), P(grp, "in"), P("in")
    matrix_in = (cols, cols, cols, rows, cols, rows)
    matrix_out = (cols, cols, rows, cols, cols, cols)
    return jax.shard_map(
        on_device,
        mesh=fine,
        in_specs=(tokens, tokens, tokens, flat, flat) + matrix_in * 4,
        out_specs=(tokens, tokens) + matrix_out * 4 + (flat, flat, flat),
        check_vma=False,
    )
```

```python
import math

import jax
import jax.numpy as jnp
import numpy as np
from jax import lax
from jax.experimental import pallas as pl
from jax.experimental.pallas import tpu as pltpu
from jax.sharding import Mesh
from jax.sharding import PartitionSpec as P

HEADS = 16
HEAD_DIM = 64
EPSILON = 1e-05
DECAY = 0.5
MOMENTUM = 0.5
RATE = 0.03
MASKED = -1e30
ROOT_TWO_PI = math.sqrt(2.0 / math.pi)
BF16 = jnp.bfloat16
F32 = jnp.float32
PLANE = ("y", "x")
CHIPS = ("y", "x", "in")
ALL = ("y", "x", "c", "in")


def dot(left, right):
    return jnp.dot(left, right, preferred_element_type=F32)


def dot_tn(left, right):
    return lax.dot_general(left, right, (((0,), (0,)), ((), ())), preferred_element_type=F32)


def dot_nt(left, right):
    return lax.dot_general(left, right, (((1,), (1,)), ((), ())), preferred_element_type=F32)


def lane_half(shape, half):
    return (lax.broadcasted_iota(jnp.int32, shape, 1) // HEAD_DIM) == half


def softmax_rows(scores):
    shifted = jnp.exp(scores - jnp.max(scores, axis=-1, keepdims=True))
    return shifted / jnp.sum(shifted, axis=-1, keepdims=True)


def attention_forward(qkv, bias):
    sequences, length, _ = bias.shape
    width = qkv.shape[1] // 3
    pair = 2 * HEAD_DIM
    scale = HEAD_DIM ** (-0.5)

    def body(qkv_ref, bias_ref, out_ref):
        for seq in range(sequences):
            rows = slice(seq * length, (seq + 1) * length)
            mask = bias_ref[seq]
            for col in range(0, width, pair):
                queries = qkv_ref[rows, col : col + pair]
                key_rows = qkv_ref[rows, width + col : width + col + pair]
                value_rows = qkv_ref[rows, 2 * width + col : 2 * width + col + pair]
                parts = []
                for half in range(2):
                    own = jnp.where(lane_half(queries.shape, half), queries, jnp.zeros_like(queries))
                    probs = softmax_rows(dot_nt(own, key_rows) * scale + mask)
                    parts.append(dot(probs.astype(BF16), value_rows))
                picked = jnp.where(lane_half(parts[0].shape, 0), parts[0], parts[1])
                out_ref[rows, col : col + pair] = picked.astype(BF16)

    return pl.pallas_call(
        body,
        out_shape=jax.ShapeDtypeStruct((qkv.shape[0], width), BF16),
        in_specs=[pl.BlockSpec(memory_space=pltpu.VMEM)] * 2,
        out_specs=pl.BlockSpec(memory_space=pltpu.VMEM),
        name="attention_forward",
    )(qkv, bias)


def attention_backward(qkv, bias, grad):
    sequences, length, _ = bias.shape
    width = qkv.shape[1] // 3
    pair = 2 * HEAD_DIM
    scale = HEAD_DIM ** (-0.5)

    def body(qkv_ref, bias_ref, grad_ref, out_ref):
        for seq in range(sequences):
            rows = slice(seq * length, (seq + 1) * length)
            mask = bias_ref[seq]
            for col in range(0, width, pair):
                queries = qkv_ref[rows, col : col + pair]
                key_rows = qkv_ref[rows, width + col : width + col + pair]
                value_rows = qkv_ref[rows, 2 * width + col : 2 * width + col + pair]
                grads = grad_ref[rows, col : col + pair]
                found = []
                for half in range(2):
                    lanes = lane_half(queries.shape, half)
                    own = jnp.where(lanes, queries, jnp.zeros_like(queries))
                    probs = softmax_rows(dot_nt(own, key_rows) * scale + mask)
                    own_grad = jnp.where(lanes, grads, jnp.zeros_like(grads))
                    grad_probs = dot_nt(own_grad, value_rows)
                    row_dot = jnp.sum(probs * grad_probs, axis=-1, keepdims=True)
                    grad_scores = (probs * (grad_probs - row_dot)).astype(BF16)
                    found.append(
                        (
                            dot(grad_scores, key_rows) * scale,
                            dot_tn(grad_scores, queries) * scale,
                            dot_tn(probs.astype(BF16), grads),
                        )
                    )
                low_lanes = lane_half((length, pair), 0)
                for third in range(3):
                    picked = jnp.where(low_lanes, found[0][third], found[1][third])
                    start = third * width + col
                    out_ref[rows, start : start + pair] = picked.astype(BF16)

    return pl.pallas_call(
        body,
        out_shape=jax.ShapeDtypeStruct(qkv.shape, BF16),
        in_specs=[pl.BlockSpec(memory_space=pltpu.VMEM)] * 3,
        out_specs=pl.BlockSpec(memory_space=pltpu.VMEM),
        name="attention_backward",
    )(qkv, bias, grad)


def whole(array):
    return pl.BlockSpec(array.shape, lambda step: (0,) * len(array.shape))


def join(pieces):
    rows, cols = pieces[0].shape

    def body(*refs):
        for k in range(len(pieces)):
            refs[-1][k * rows : (k + 1) * rows, :] = refs[k][...]

    in_vmem = pl.BlockSpec(memory_space=pltpu.VMEM)
    return pl.pallas_call(
        body,
        out_shape=jax.ShapeDtypeStruct((len(pieces) * rows, cols), pieces[0].dtype),
        in_specs=[in_vmem] * len(pieces),
        out_specs=in_vmem,
        name="join",
    )(*pieces)


def first_kernel(normed, heads, attended, branch, numbers, distances, dtype):
    width, chips = normed.shape[1], numbers.shape[0] - 2
    cols, pair = heads.shape[1] // chips, branch.shape[1] // chips
    rows, share = width // chips, pair // 2
    tall = attended.shape[1] // chips

    def body(number_ref, normed_ref, heads_ref, attended_ref, branch_ref, *targets):
        for d, target in zip(distances, targets):
            chip = number_ref[2 + d]
            head = heads_ref[:, pl.ds(pl.multiple_of(chip * cols, cols), cols)]
            target[:, :cols] = dot_tn(normed_ref[...], head).astype(dtype)
            term = branch_ref[:, pl.ds(pl.multiple_of(chip * pair, pair), pair)]
            term = dot_tn(attended_ref[...], term).astype(dtype)
            for k in range(chips):
                for half in range(2):
                    start = k * rows + half * tall
                    target[start : start + tall, cols:] = term[
                        k * tall : (k + 1) * tall, half * share : (half + 1) * share
                    ]

    in_vmem = pl.BlockSpec(memory_space=pltpu.VMEM)
    return pl.pallas_call(
        body,
        out_shape=[jax.ShapeDtypeStruct((width, cols + share), dtype)] * len(distances),
        in_specs=[pl.BlockSpec(memory_space=pltpu.SMEM)] + [in_vmem] * 4,
        out_specs=[in_vmem] * len(distances),
        name="first_terms",
    )(numbers, normed, heads, attended, branch)


def column_kernel(own, blocks, parts, numbers):
    width = own.shape[0]
    count, _, rows, share = blocks.shape
    chunks = width // rows
    sizes = [root.shape[0] for _, root in parts]
    total = sum(sizes)
    used = len(parts)

    def body(number_ref, own_ref, *refs):
        block_refs, right_refs = refs[:used], refs[used : 2 * used]
        mine_ref, theirs_ref, left_ref = refs[2 * used :]
        core, depth = number_ref[0], number_ref[1]
        near = pl.ds(pl.multiple_of(depth * rows, rows), rows)

        @pl.loop(0, chunks)
        def _(d):
            chunk = number_ref[2 + d]
            span = pl.ds(pl.multiple_of(d * rows, rows), rows)
            first = 0
            for k, cols in enumerate(sizes):
                lanes = slice(first, first + cols)
                for g in range(count // chunks):
                    left_ref[:, g * share : (g + 1) * share] = block_refs[k][g * chunks + chunk, 0]
                image = dot(left_ref[...], own_ref[:, lanes]).astype(BF16)
                for pick, target in ((core, mine_ref), (1 - core, theirs_ref)):
                    right = right_refs[k][:, pl.ds(pl.multiple_of(pick * cols, cols), cols)]
                    target[span, lanes] = dot(image, right.astype(BF16)).astype(target.dtype)
                    start = pl.multiple_of(chunk * rows + pick * share, share)
                    left = dot_nt(own_ref[near, lanes], own_ref[pl.ds(start, share), lanes])
                    low = total + k * share
                    target[span, low : low + share] = left.astype(target.dtype)
                first += cols

    shape = (width, total + used * share)
    return pl.pallas_call(
        body,
        grid=(1,),
        out_shape=(jax.ShapeDtypeStruct(shape, F32), jax.ShapeDtypeStruct(shape, BF16)),
        in_specs=[pl.BlockSpec(memory_space=pltpu.SMEM), whole(own)]
        + [
            pl.BlockSpec((count, 1, rows, share), lambda step, which=which: (0, which, 0, 0))
            for which, _ in parts
        ]
        + [whole(root) for _, root in parts],
        out_specs=(pl.BlockSpec(shape, lambda step: (0, 0)),) * 2,
        scratch_shapes=[pltpu.VMEM((rows, width), BF16)],
        compiler_params=pltpu.CompilerParams(vmem_limit_bytes=40 << 20),
        name="column_terms",
    )(numbers, own, *[blocks] * used, *[root for _, root in parts])


def row_kernel(own, blocks, which, left_root, numbers):
    width, count = own.shape
    devices, _, rows, share = blocks.shape
    chunks = width // rows
    tall = left_root.shape[0]
    piece = tall + 2 * share

    def body(number_ref, own_ref, block_ref, left_ref, mine_ref, theirs_ref, right_ref):
        core, depth = number_ref[0], number_ref[1]
        targets = ((core, mine_ref), (1 - core, theirs_ref))
        near = own_ref[pl.ds(pl.multiple_of(depth * rows, rows), rows), :]
        for d in range(chunks):
            chunk = number_ref[2 + d]
            for k, (pick, target) in enumerate(targets):
                part = pl.ds(pl.multiple_of(pick * share, share), share)
                lanes = slice((k * chunks + d) * share, (k * chunks + d + 1) * share)
                for g in range(devices // chunks):
                    right_ref[g * share : (g + 1) * share, lanes] = block_ref[
                        g * chunks + chunk, 0, part, :
                    ]
                start = pl.multiple_of(chunk * rows + pick * share, share)
                right = dot_nt(own_ref[pl.ds(start, share), :], near).astype(target.dtype)
                low = d * piece + tall
                target[low : low + share, :] = right[:, :share]
                target[low + share : low + 2 * share, :] = right[:, share:]
        for first in range(0, tall, rows):
            image = dot_nt(left_ref[first : first + rows, :].astype(BF16), own_ref[...])
            ahead = dot(image.astype(BF16), right_ref[...])
            for k, (_, target) in enumerate(targets):
                for d in range(chunks):
                    lanes = slice((k * chunks + d) * share, (k * chunks + d + 1) * share)
                    low = d * piece + first
                    target[low : low + rows, :] = ahead[:, lanes].astype(target.dtype)

    shape = (chunks * piece, share)
    return pl.pallas_call(
        body,
        grid=(1,),
        out_shape=(jax.ShapeDtypeStruct(shape, F32), jax.ShapeDtypeStruct(shape, BF16)),
        in_specs=[
            pl.BlockSpec(memory_space=pltpu.SMEM),
            whole(own),
            pl.BlockSpec((devices, 1, rows, share), lambda step: (0, which, 0, 0)),
            whole(left_root),
        ],
        out_specs=(pl.BlockSpec(shape, lambda step: (0, 0)),) * 2,
        scratch_shapes=[pltpu.VMEM((width, width), BF16)],
        compiler_params=pltpu.CompilerParams(vmem_limit_bytes=40 << 20),
        name="row_terms",
    )(numbers, own, blocks, left_root)


class Place:
    def __init__(self):
        self.rows = lax.axis_size("y")
        self.plane = self.rows * lax.axis_size("x")
        self.depth = lax.axis_size("in")
        self.q = lax.axis_index("y") * lax.axis_size("x") + lax.axis_index("x")
        self.c = lax.axis_index("c")
        self.z = lax.axis_index("in")
        self.last = {}

    def send(self, values, axes, pairs, lane=None):
        if lane in self.last:
            values, _ = lax.optimization_barrier((values, self.last[lane]))
        values = [lax.ppermute(value, axes, pair) for value, pair in zip(values, pairs)]
        if lane is not None:
            self.last[lane] = values
        return values

    def after(self, value, *earlier):
        return lax.optimization_barrier((value, *earlier))[0]

    def all_after(self, values, *earlier):
        return lax.optimization_barrier((tuple(values), *earlier))[0]

    def swap_core(self, value):
        return self.send([value], "c", [[(0, 1), (1, 0)]])[0]

    def swap_plane(self, values, distances, lane="plane"):
        pairs = [[(k, k ^ d) for k in range(self.plane)] for d in distances]
        return self.send(values, PLANE, pairs, lane)

    def on_depth(self, value):
        if "depth" in self.last:
            value, _ = lax.optimization_barrier((value, self.last["depth"]))
        value = lax.all_to_all(value, "in", 0, 0, tiled=True)
        self.last["depth"] = value
        return value

    def on_chips(self, values, targets, lane):
        pairs = []
        for target in targets:
            found = [
                (q, z, target(q, z))
                for q in range(self.plane)
                for z in range(self.depth)
                if target(q, z) is not None
            ]
            pairs.append([(q * self.depth + z, t[0] * self.depth + t[1]) for q, z, t in found])
        return self.send(values, CHIPS, pairs, lane)

    def by_core(self, own, other):
        return jnp.where(self.c == 0, own, other), jnp.where(self.c == 0, other, own)

    def mine(self, pair):
        return jnp.where(self.c == 0, pair[0], pair[1])

    def theirs(self, pair):
        return jnp.where(self.c == 0, pair[1], pair[0])

    def shuffle(self, values, index):
        values = list(values)
        bit = 1
        while bit < len(values):
            on = (index // bit) % 2 == 1
            values = [jnp.where(on, values[k ^ bit], values[k]) for k in range(len(values))]
            bit *= 2
        return values

    def gather_depth(self, value):
        return self.on_depth(jnp.broadcast_to(value[None], (self.depth,) + value.shape))

    def transpose_chips(self, value, lane):
        return self.on_chips([value], [lambda q, z: (z, q)], lane)[0]

    def spread_plane(self, value):
        q, z = self.q, self.z
        if self.plane != 4:
            total = jnp.where(q == z, value, jnp.zeros_like(value))
            targets = [
                lambda a, b, d=d: (a ^ d, b) if a == b else None for d in range(1, self.plane)
            ]
            for part in self.on_chips([value] * len(targets), targets, "plane"):
                total = total + part
            return total
        half = value.shape[0] // 2
        low, high = value[:half], value[half:]
        low_x, high_y = self.on_chips(
            [low, high],
            [
                lambda a, b: (a ^ 1, b) if a == b else None,
                lambda a, b: (a ^ 2, b) if a == b else None,
            ],
            "plane",
        )
        high_x, low_y = self.on_chips(
            [jnp.where(q == z, high, high_y), jnp.where(q == z, low, low_x)],
            [
                lambda a, b: (a ^ 1, b) if a ^ b in (0, 2) else None,
                lambda a, b: (a ^ 2, b) if a ^ b in (0, 1) else None,
            ],
            "plane",
        )
        apart = q ^ z
        low = jnp.where(apart == 0, low, jnp.where(apart == 1, low_x, low_y))
        high = jnp.where(apart == 0, high, jnp.where(apart == 2, high_y, high_x))
        return jnp.concatenate([low, high])

    def gather_tokens(self, value):
        mine = self.gather_plane(value)
        return join(mine + [self.swap_core(part) for part in mine])

    def reduce_tokens(self, mine, theirs):
        total = mine + self.swap_core(theirs.astype(BF16)).astype(F32)
        return self.reduce_plane(jnp.split(total, self.plane))

    def by_two_steps(self, shape):
        return self.plane == 4 and math.prod(shape) > 200_000

    def gather_plane(self, value):
        if not self.by_two_steps(value.shape):
            others = range(1, self.plane)
            return [value] + self.swap_plane([value] * len(others), others)
        half = value.shape[0] // 2
        by_x, by_y = self.swap_plane([value, value], (1, 2))
        first, second = self.swap_plane([by_y[:half], by_x[half:]], (1, 2))
        return [value, by_x, by_y, jnp.concatenate([first, second])]

    def reduce_plane(self, values):
        total = values[0]
        others = [value.astype(BF16) for value in values[1:]]
        for part in self.swap_plane(others, range(1, self.plane)):
            total = total + part.astype(F32)
        return total

    def reduce_plane_late(self, far, rest):
        if self.plane != 4:
            return self.reduce_plane([*rest(), far])
        half = far.shape[0] // 2
        first, second = self.swap_plane([far[:half], far[half:]], (1, 2))
        own, to_x, to_y = rest()
        to_y = jnp.concatenate([to_y[:half] + first.astype(F32), to_y[half:]])
        to_x = jnp.concatenate([to_x[:half], to_x[half:] + second.astype(F32)])
        by_x, by_y = self.swap_plane([to_x.astype(BF16), to_y.astype(BF16)], (1, 2))
        return own + by_x.astype(F32) + by_y.astype(F32)


def norm_parts(values):
    centred = values - jnp.mean(values, axis=-1, keepdims=True)
    spread = lax.rsqrt(jnp.mean(centred * centred, axis=-1, keepdims=True) + EPSILON)
    return centred * spread, spread


def norm_backward(grad, scaled, spread, gain):
    inner = grad * gain
    mean_one = jnp.mean(inner, axis=-1, keepdims=True)
    mean_two = jnp.mean(inner * scaled, axis=-1, keepdims=True)
    return spread * (inner - mean_one - scaled * mean_two)


def gelu(values):
    return 0.5 * values * (1.0 + jnp.tanh(ROOT_TWO_PI * (values + 0.044715 * values**3)))


def gelu_slope(values):
    squared = values * values
    bent = jnp.tanh(ROOT_TWO_PI * (values + 0.044715 * squared * values))
    return 0.5 * (1.0 + bent) + 0.5 * values * (1.0 - bent * bent) * (
        ROOT_TWO_PI * (1.0 + 3.0 * 0.044715 * squared)
    )


def on_device(
    tokens,
    segments,
    cotangent,
    vectors,
    vector_moment,
    qkv_weight,
    qkv_moment,
    qkv_left,
    qkv_right,
    qkv_left_root,
    qkv_right_root,
    out_weight,
    out_moment,
    out_left,
    out_right,
    out_left_root,
    out_right_root,
    fc_weight,
    fc_moment,
    fc_left,
    fc_right,
    fc_left_root,
    fc_right_root,
    proj_weight,
    proj_moment,
    proj_left,
    proj_right,
    proj_left_root,
    proj_right_root,
):
    here = Place()
    plane, depth = here.plane, here.depth
    length, width = tokens.shape
    z, q, c = here.z, here.q, here.c
    block = 2 * HEAD_DIM if qkv_weight.shape[1] % (2 * HEAD_DIM) == 0 else HEAD_DIM

    def far_columns(own):
        far = here.spread_plane(own)
        return here.by_core(far, here.swap_core(far))

    def pair_columns(share):
        return jnp.concatenate(here.by_core(share, here.swap_core(share)), axis=1)

    def by_parity(pair):
        parts = jnp.split(pair, pair.shape[1] // block, axis=1)
        return jnp.concatenate([here.mine(parts[k : k + 2]) for k in range(0, len(parts), 2)], axis=1)

    qkv_share = by_parity(pair_columns(qkv_weight.astype(BF16)))
    fc_share = fc_weight.astype(BF16)
    proj_split = proj_weight.astype(BF16).reshape(2, -1, proj_weight.shape[1])
    proj_share = jnp.concatenate(
        here.by_core(here.mine(proj_split), here.swap_core(here.theirs(proj_split))), axis=1
    )
    out_split = out_weight.astype(BF16).reshape(-1, 2, block, out_weight.shape[1])
    out_split = (
        out_split[:, 0].reshape(-1, out_weight.shape[1]),
        out_split[:, 1].reshape(-1, out_weight.shape[1]),
    )
    out_share = jnp.concatenate(
        here.by_core(here.mine(out_split), here.swap_core(here.theirs(out_split))), axis=1
    )

    proj_turned = here.transpose_chips(proj_share.T, "plane")
    plane_cotangent = here.gather_tokens(cotangent)
    qkv_parts = here.gather_plane(here.gather_depth(qkv_share).reshape(width, -1))
    small_share = jnp.concatenate(
        [out_share, vectors.astype(BF16).reshape(-1, out_share.shape[1])]
    )
    small_whole = here.gather_depth(small_share)
    vector_whole = small_whole[:, out_share.shape[0] :].reshape(-1)
    out_rows = small_whole[:, : out_share.shape[0]].reshape(-1, out_share.shape[1])
    out_full = jnp.concatenate(here.shuffle(here.gather_plane(out_rows), q), axis=1)
    fc_full = here.gather_depth(fc_share).reshape(width, -1)
    proj_full = here.gather_depth(proj_turned).reshape(width, -1)

    numbers = jnp.stack([c, z] + [q ^ d for d in range(plane)]).astype(jnp.int32)

    params = vector_whole.astype(F32)
    unit = fc_weight.shape[1]
    hidden = unit * 2 * plane
    gain_one, shift_one, bias_query, bias_value, bias_out, gain_two, shift_two = (
        params[k * width : (k + 1) * width] for k in range(7)
    )
    bias_fc = lax.dynamic_slice_in_dim(params, 7 * width + (2 * q + c) * unit, unit)
    bias_proj = params[7 * width + hidden :]

    pair_tokens = jnp.concatenate([tokens, here.swap_core(tokens)])
    labels = jnp.concatenate([segments, here.swap_core(segments)])
    position = jnp.arange(length)
    allowed = (labels[:, :, None] == labels[:, None, :]) & (position[:, None] >= position[None, :])
    mask = jnp.where(allowed, 0.0, MASKED).astype(F32)

    inputs = pair_tokens.astype(F32)
    scaled_one, spread_one = norm_parts(inputs)
    normed_one = (scaled_one * gain_one + shift_one).astype(BF16)
    qkv_bias = jnp.concatenate([bias_query, jnp.zeros_like(bias_query), bias_value])
    qkv_bias = qkv_bias.reshape(-1, 2, block)
    qkv_bias = here.mine((qkv_bias[:, 0], qkv_bias[:, 1])).reshape(-1)
    projected = jnp.concatenate(
        here.shuffle([dot(normed_one, part) for part in qkv_parts], q), axis=1
    )
    projected = (projected + qkv_bias).astype(BF16)
    share_rows, share_cols = qkv_left_root.shape
    right_root = proj_right_root.astype(BF16)
    root_blocks = lax.all_gather(
        here.after(
            jnp.stack(
                [root.astype(BF16) for root in (qkv_left_root, out_left_root, fc_left_root)]
                + [jnp.concatenate([right_root[:, :share_cols], right_root[:, share_cols:]])]
            ),
            projected,
        ),
        ALL,
    )
    attended = attention_forward(projected, mask)
    attended = here.after(attended, plane_cotangent, fc_full)
    branch = dot(attended[:length], out_full) + here.swap_core(dot(attended[length:], out_full))
    middle = inputs[:length] + (branch + bias_out)
    scaled_two, spread_two = norm_parts(middle)
    normed_two = here.gather_tokens((scaled_two * gain_two + shift_two).astype(BF16))
    normed_two = here.after(normed_two, proj_full)
    pre_act = dot(normed_two, fc_full) + bias_fc
    activated = gelu(pre_act).astype(BF16)

    token_total = length * 2 * plane * depth
    factor = 1.0 / math.sqrt(token_total)
    half = plane * length
    proj_terms = dot_tn(plane_cotangent, activated)
    proj_parts = here.on_depth(proj_terms.reshape(depth, -1, unit).astype(BF16))
    late_cotangent = here.after(plane_cotangent, proj_terms)
    grad_pre = (dot(late_cotangent, proj_full) * gelu_slope(pre_act)).astype(BF16)
    two_mine, two_theirs = dot_nt(grad_pre[:half], fc_full), dot_nt(grad_pre[half:], fc_full)
    grad_normed_two = here.reduce_tokens(two_mine, two_theirs)
    fc_terms = dot_tn(here.after(normed_two, two_mine, two_theirs), grad_pre)

    grad_top = cotangent.astype(F32)
    grad_middle = grad_top + norm_backward(grad_normed_two, scaled_two, spread_two, gain_two)
    own_branch = grad_middle.astype(BF16)
    grad_branch = jnp.concatenate([own_branch, here.swap_core(own_branch)])

    def total(parts):
        return jnp.sum(parts.astype(F32), axis=0) * factor

    proj_sum = total(here.after(proj_parts, own_branch))
    fc_grad = total(
        here.on_depth(here.after(fc_terms.reshape(depth, -1, unit).astype(BF16), own_branch))
    )

    fc_own = here.gather_depth(fc_grad.astype(BF16)).reshape(width, -1)

    grad_attended = dot_nt(grad_branch, out_full).astype(BF16)
    grad_heads = attention_backward(projected, mask, grad_attended)

    rows_own, qkv_cols = qkv_weight.shape
    out_cols = out_weight.shape[1]
    aligned = out_cols % 128 == 0
    head_blocks = here.shuffle(jnp.split(grad_heads, plane, axis=1), q)

    def first_terms(distances, dtype):
        if aligned:
            return first_kernel(
                normed_one, grad_heads, attended, grad_branch, numbers, distances, dtype
            )
        found = []
        for d in distances:
            block = lax.dynamic_slice_in_dim(grad_branch, (q ^ d) * 2 * out_cols, 2 * out_cols, 1)
            term = dot_tn(attended, block).reshape(depth, -1, 2 * out_cols)
            term = jnp.concatenate([term[:, :, :out_cols], term[:, :, out_cols:]], axis=1)
            term = term.reshape(width, out_cols)
            head = dot_tn(normed_one, head_blocks[d])
            found.append(jnp.concatenate([head, term], axis=1).astype(dtype))
        return found

    def second_terms():
        own, *rest = first_terms(tuple(range(plane - 1)), F32)
        return own, *here.all_after(rest, fc_grad)

    first_parts_ready = here.reduce_plane_late(
        first_terms((plane - 1,), BF16)[0], second_terms
    ).astype(BF16)
    first_parts = here.on_depth(first_parts_ready.reshape(depth, -1, qkv_cols + out_cols))

    other_one = sum(dot_nt(part[length:], rows) for part, rows in zip(head_blocks, qkv_parts))
    grad_normed_one = sum(dot_nt(part[:length], rows) for part, rows in zip(head_blocks, qkv_parts))
    grad_normed_one = grad_normed_one + here.swap_core(other_one)
    own_scaled = scaled_one[:length]
    grad_in = norm_backward(grad_normed_one, own_scaled, spread_one[:length], gain_one)
    input_grad = (grad_middle + grad_in).astype(BF16)

    def sum_over_group(mine, theirs):
        return here.reduce_plane(jnp.split(mine + here.swap_core(theirs).astype(F32), plane))

    def column_terms(own, parts):
        if aligned:
            return column_kernel(own, root_blocks, parts, numbers)
        first, found = 0, []
        for which, right_root in parts:
            cols = right_root.shape[0]
            piece = own[:, first : first + cols]
            first += cols
            blocks = root_blocks.reshape(2 * plane, depth, 4, share_rows, share_cols)[:, :, which]
            left_root = blocks.transpose(1, 2, 0, 3).reshape(depth, share_rows, width)
            left_root = jnp.concatenate(here.shuffle(list(left_root), q))
            image = dot(left_root, piece).astype(BF16)
            right_halves = jnp.split(right_root.astype(BF16), 2, axis=1)
            left = dot_nt(lax.dynamic_slice_in_dim(piece, z * rows_own, rows_own), piece)
            left = here.shuffle(jnp.split(left, plane, axis=1), q)
            left = jnp.split(jnp.concatenate(left), 2, axis=1)
            found.append(
                [(dot(image, pick(right_halves)), pick(left)) for pick in (here.mine, here.theirs)]
            )
        mine, theirs = (
            jnp.concatenate([one[k][0] for one in found] + [one[k][1] for one in found], axis=1)
            for k in range(2)
        )
        return mine, theirs.astype(BF16)

    def row_terms(own, which, left_root):
        if aligned:
            return row_kernel(own, root_blocks, which, left_root, numbers)
        blocks = root_blocks.reshape(2 * plane, depth, 4, 2, share_rows // 2, share_cols)[:, :, which]
        chunk = width // depth
        right = dot_nt(own, lax.dynamic_slice_in_dim(own, z * chunk, chunk))
        right = here.shuffle(jnp.split(right, plane), q)
        image = dot_nt(left_root.astype(BF16), own).astype(BF16)
        found = []
        for pick in (here.mine, here.theirs):
            root = pick((blocks[:, :, 0], blocks[:, :, 1]))
            root = [root[:, r].reshape(width, share_cols) for r in range(depth)]
            root = jnp.concatenate(here.shuffle(root, q), axis=1)
            ahead = jnp.split(dot(image, root), plane, axis=1)
            stats = [
                jnp.concatenate(jnp.split(pick(jnp.split(pair, 2)), 2, axis=1)) for pair in right
            ]
            found.append(
                jnp.concatenate([jnp.concatenate(parts) for parts in zip(ahead, stats)])
            )
        return found[0], found[1].astype(BF16)

    fc_mine, fc_theirs = column_terms(fc_own, [(2, fc_right_root)])
    fc_other = here.swap_core(fc_theirs)
    fc_total = here.reduce_plane(jnp.split(fc_mine + fc_other.astype(F32), plane))
    first_sum = total(here.after(first_parts, fc_total))

    qkv_parity = first_sum[:, :qkv_cols]
    qkv_other = here.swap_core(qkv_parity)
    qkv_pair = []
    for k in range(0, qkv_cols, block):
        qkv_pair += here.by_core(qkv_parity[:, k : k + block], qkv_other[:, k : k + block])
    half_count = len(qkv_pair) // 2
    qkv_grad = jnp.concatenate(
        [here.mine((qkv_pair[k], qkv_pair[k + half_count])) for k in range(half_count)], axis=1
    )
    out_halves = jnp.split(first_sum[:, qkv_cols:], 2)
    out_pair = here.by_core(here.mine(out_halves), here.swap_core(here.theirs(out_halves)))
    out_grad = jnp.stack(
        [part.reshape(-1, block, out_cols) for part in out_pair], axis=1
    ).reshape(out_weight.shape)
    first_low = jnp.concatenate([qkv_grad, out_grad], axis=1).astype(BF16)
    first_own = here.gather_depth(first_low).reshape(width, -1)

    fc_far = far_columns(here.after(fc_own, first_low))

    late_activated = here.after(activated, first_low)
    output = here.reduce_tokens(
        dot_nt(late_activated[:half], proj_full), dot_nt(late_activated[half:], proj_full)
    )
    output = (middle + (output + bias_proj)).astype(BF16)

    first_total = sum_over_group(
        *column_terms(here.after(first_own, fc_far[0], output), [(0, qkv_right_root), (1, out_right_root)])
    )

    proj_own = here.gather_depth(proj_sum.astype(BF16)).reshape(width, -1)
    unit_cols = fc_weight.shape[1]
    first_far = far_columns(first_own)
    proj_total = sum_over_group(*row_terms(proj_own, 3, proj_left_root))
    proj_far = far_columns(proj_own)
    own_cols = proj_weight.shape[1]
    proj_grad = jnp.concatenate(
        [
            lax.dynamic_slice_in_dim(part, (2 * q + c) * own_cols, own_cols).T
            for part in proj_far
        ]
    ).astype(F32)
    proj_left_sum = dot_tn(jnp.concatenate(proj_far, axis=1), proj_own)

    def interleave(value):
        value = value.reshape(-1, 1, block)
        zeros = jnp.zeros_like(value)
        return jnp.concatenate(here.by_core(value, zeros), axis=1).reshape(-1)

    head_sums = interleave(jnp.sum(grad_heads.astype(F32), axis=0))
    fc_bias_terms = lax.dynamic_update_slice_in_dim(
        jnp.zeros((hidden,), F32), jnp.sum(grad_pre.astype(F32), axis=0), (2 * q + c) * unit, 0
    )
    vector_terms = jnp.concatenate(
        [
            jnp.sum(grad_normed_one * own_scaled, axis=0),
            jnp.sum(grad_normed_one, axis=0),
            head_sums[:width],
            head_sums[2 * width :],
            jnp.sum(own_branch.astype(F32), axis=0),
            jnp.sum(grad_normed_two * scaled_two, axis=0),
            jnp.sum(grad_normed_two, axis=0),
            fc_bias_terms,
            jnp.sum(grad_top, axis=0),
        ]
    )
    vector_sum = here.swap_core(vector_terms) + vector_terms
    vector_sum = jnp.sum(here.on_depth(vector_sum.reshape(depth, -1, 128)), axis=0)
    distance = 1
    while distance < plane:
        vector_sum = vector_sum + here.swap_plane([vector_sum], [distance], None)[0]
        distance *= 2
    vector_grad = vector_sum.reshape(-1) * factor

    cut = qkv_cols + out_cols
    first_direction = here.transpose_chips(first_total[:, :cut].astype(BF16), "turn").astype(F32)
    fc_direction = here.transpose_chips(fc_total[:, :unit_cols].astype(BF16), "turn").astype(F32)
    qkv_direction, out_direction = first_direction[:, :qkv_cols], first_direction[:, qkv_cols:]
    qkv_left_sum = first_total[:, cut : cut + out_cols]
    out_left_sum = first_total[:, cut + out_cols :]
    fc_left_sum = fc_total[:, unit_cols:]
    proj_direction = proj_total[: proj_weight.shape[0]]
    proj_right_sum = jnp.concatenate(jnp.split(proj_total[proj_weight.shape[0] :], 2), axis=1)

    fc_right_sum = dot_tn(fc_own, jnp.concatenate(fc_far, axis=1))
    qkv_right_sum = dot_tn(
        first_own[:, :qkv_cols], jnp.concatenate([part[:, :qkv_cols] for part in first_far], axis=1)
    )
    out_right_sum = dot_tn(
        first_own[:, qkv_cols:], jnp.concatenate([part[:, qkv_cols:] for part in first_far], axis=1)
    )

    results = []
    for grad, weight, moment, left, right, found, row_total, col_total in (
        (
            qkv_grad,
            qkv_weight,
            qkv_moment,
            qkv_left,
            qkv_right,
            (qkv_left_sum, qkv_right_sum, qkv_direction),
            width,
            3 * width,
        ),
        (
            out_grad,
            out_weight,
            out_moment,
            out_left,
            out_right,
            (out_left_sum, out_right_sum, out_direction),
            width,
            width,
        ),
        (
            fc_grad,
            fc_weight,
            fc_moment,
            fc_left,
            fc_right,
            (fc_left_sum, fc_right_sum, fc_direction),
            width,
            hidden,
        ),
        (
            proj_grad,
            proj_weight,
            proj_moment,
            proj_left,
            proj_right,
            (proj_left_sum, proj_right_sum, proj_direction),
            hidden,
            width,
        ),
    ):
        left_sum, right_sum, direction = found
        new_moment = MOMENTUM * moment + direction
        new_weight = weight - RATE * new_moment
        results += [
            grad,
            DECAY * left + (1.0 - DECAY) / col_total * left_sum,
            DECAY * right + (1.0 - DECAY) / row_total * right_sum,
            new_moment,
            new_weight,
            new_weight.astype(BF16),
        ]
    new_vector_moment = MOMENTUM * vector_moment + vector_grad
    new_vectors = vectors - RATE * new_vector_moment
    return (output, input_grad, *results, vector_grad, new_vector_moment, new_vectors)


def solution(mesh):
    groups, depth = mesh.shape["grp"], mesh.shape["in"]
    fine = Mesh(mesh.devices.reshape(groups // 4, 2, 2, depth), ALL)
    grp = ("y", "x", "c")
    tokens, cols, rows, flat = P(ALL, None), P("in", grp), P(grp, "in"), P("in")
    matrix_in = (cols, cols, cols, rows, cols, rows)
    matrix_out = (cols, cols, rows, cols, cols, cols)
    return jax.shard_map(
        on_device,
        mesh=fine,
        in_specs=(tokens, tokens, tokens, flat, flat) + matrix_in * 4,
        out_specs=(tokens, tokens) + matrix_out * 4 + (flat, flat, flat),
        check_vma=False,
    )
```

```python
import math

import jax
import jax.numpy as jnp
import numpy as np
from jax import lax
from jax.experimental import pallas as pl
from jax.experimental.pallas import tpu as pltpu
from jax.sharding import Mesh
from jax.sharding import PartitionSpec as P

HEADS = 16
HEAD_DIM = 64
EPSILON = 1e-05
DECAY = 0.5
MOMENTUM = 0.5
RATE = 0.03
MASKED = -1e30
ROOT_TWO_PI = math.sqrt(2.0 / math.pi)
BF16 = jnp.bfloat16
F32 = jnp.float32
PLANE = ("y", "x")
CHIPS = ("y", "x", "in")
ALL = ("y", "x", "c", "in")


def dot(left, right):
    return jnp.dot(left, right, preferred_element_type=F32)


def dot_tn(left, right):
    return lax.dot_general(left, right, (((0,), (0,)), ((), ())), preferred_element_type=F32)


def dot_nt(left, right):
    return lax.dot_general(left, right, (((1,), (1,)), ((), ())), preferred_element_type=F32)


def lane_half(shape, half):
    return (lax.broadcasted_iota(jnp.int32, shape, 1) // HEAD_DIM) == half


def softmax_rows(scores):
    shifted = jnp.exp(scores - jnp.max(scores, axis=-1, keepdims=True))
    return shifted / jnp.sum(shifted, axis=-1, keepdims=True)


def attention_forward(qkv, bias):
    sequences, length, _ = bias.shape
    width = qkv.shape[1] // 3
    pair = 2 * HEAD_DIM
    scale = HEAD_DIM ** (-0.5)

    def body(qkv_ref, bias_ref, out_ref):
        for seq in range(sequences):
            rows = slice(seq * length, (seq + 1) * length)
            mask = bias_ref[seq]
            for col in range(0, width, pair):
                queries = qkv_ref[rows, col : col + pair]
                key_rows = qkv_ref[rows, width + col : width + col + pair]
                value_rows = qkv_ref[rows, 2 * width + col : 2 * width + col + pair]
                parts = []
                for half in range(2):
                    own = jnp.where(lane_half(queries.shape, half), queries, jnp.zeros_like(queries))
                    probs = softmax_rows(dot_nt(own, key_rows) * scale + mask)
                    parts.append(dot(probs.astype(BF16), value_rows))
                picked = jnp.where(lane_half(parts[0].shape, 0), parts[0], parts[1])
                out_ref[rows, col : col + pair] = picked.astype(BF16)

    return pl.pallas_call(
        body,
        out_shape=jax.ShapeDtypeStruct((qkv.shape[0], width), BF16),
        in_specs=[pl.BlockSpec(memory_space=pltpu.VMEM)] * 2,
        out_specs=pl.BlockSpec(memory_space=pltpu.VMEM),
        name="attention_forward",
    )(qkv, bias)


def attention_backward(qkv, bias, grad):
    sequences, length, _ = bias.shape
    width = qkv.shape[1] // 3
    pair = 2 * HEAD_DIM
    scale = HEAD_DIM ** (-0.5)

    def body(qkv_ref, bias_ref, grad_ref, out_ref):
        for seq in range(sequences):
            rows = slice(seq * length, (seq + 1) * length)
            mask = bias_ref[seq]
            for col in range(0, width, pair):
                queries = qkv_ref[rows, col : col + pair]
                key_rows = qkv_ref[rows, width + col : width + col + pair]
                value_rows = qkv_ref[rows, 2 * width + col : 2 * width + col + pair]
                grads = grad_ref[rows, col : col + pair]
                found = []
                for half in range(2):
                    lanes = lane_half(queries.shape, half)
                    own = jnp.where(lanes, queries, jnp.zeros_like(queries))
                    probs = softmax_rows(dot_nt(own, key_rows) * scale + mask)
                    own_grad = jnp.where(lanes, grads, jnp.zeros_like(grads))
                    grad_probs = dot_nt(own_grad, value_rows)
                    row_dot = jnp.sum(probs * grad_probs, axis=-1, keepdims=True)
                    grad_scores = (probs * (grad_probs - row_dot)).astype(BF16)
                    found.append(
                        (
                            dot(grad_scores, key_rows) * scale,
                            dot_tn(grad_scores, queries) * scale,
                            dot_tn(probs.astype(BF16), grads),
                        )
                    )
                low_lanes = lane_half((length, pair), 0)
                for third in range(3):
                    picked = jnp.where(low_lanes, found[0][third], found[1][third])
                    start = third * width + col
                    out_ref[rows, start : start + pair] = picked.astype(BF16)

    return pl.pallas_call(
        body,
        out_shape=jax.ShapeDtypeStruct(qkv.shape, BF16),
        in_specs=[pl.BlockSpec(memory_space=pltpu.VMEM)] * 3,
        out_specs=pl.BlockSpec(memory_space=pltpu.VMEM),
        name="attention_backward",
    )(qkv, bias, grad)


def whole(array):
    return pl.BlockSpec(array.shape, lambda step: (0,) * len(array.shape))


def join(pieces):
    rows, cols = pieces[0].shape

    def body(*refs):
        for k in range(len(pieces)):
            refs[-1][k * rows : (k + 1) * rows, :] = refs[k][...]

    in_vmem = pl.BlockSpec(memory_space=pltpu.VMEM)
    return pl.pallas_call(
        body,
        out_shape=jax.ShapeDtypeStruct((len(pieces) * rows, cols), pieces[0].dtype),
        in_specs=[in_vmem] * len(pieces),
        out_specs=in_vmem,
        name="join",
    )(*pieces)


def first_kernel(normed, heads, attended, branch, numbers, distances, dtype):
    width, chips = normed.shape[1], numbers.shape[0] - 2
    cols, pair = heads.shape[1] // chips, branch.shape[1] // chips
    rows, share = width // chips, pair // 2
    tall = attended.shape[1] // chips

    def body(number_ref, normed_ref, heads_ref, attended_ref, branch_ref, *targets):
        for d, target in zip(distances, targets):
            chip = number_ref[2 + d]
            head = heads_ref[:, pl.ds(pl.multiple_of(chip * cols, cols), cols)]
            target[:, :cols] = dot_tn(normed_ref[...], head).astype(dtype)
            term = branch_ref[:, pl.ds(pl.multiple_of(chip * pair, pair), pair)]
            term = dot_tn(attended_ref[...], term).astype(dtype)
            for k in range(chips):
                for half in range(2):
                    start = k * rows + half * tall
                    target[start : start + tall, cols:] = term[
                        k * tall : (k + 1) * tall, half * share : (half + 1) * share
                    ]

    in_vmem = pl.BlockSpec(memory_space=pltpu.VMEM)
    return pl.pallas_call(
        body,
        out_shape=[jax.ShapeDtypeStruct((width, cols + share), dtype)] * len(distances),
        in_specs=[pl.BlockSpec(memory_space=pltpu.SMEM)] + [in_vmem] * 4,
        out_specs=[in_vmem] * len(distances),
        name="first_terms",
    )(numbers, normed, heads, attended, branch)


def column_kernel(own, blocks, parts, numbers):
    width = own.shape[0]
    count, _, rows, share = blocks.shape
    chunks = width // rows
    sizes = [root.shape[0] for _, root in parts]
    total = sum(sizes)
    used = len(parts)

    def body(number_ref, own_ref, *refs):
        block_refs, right_refs = refs[:used], refs[used : 2 * used]
        mine_ref, theirs_ref, left_ref = refs[2 * used :]
        core, depth = number_ref[0], number_ref[1]
        near = pl.ds(pl.multiple_of(depth * rows, rows), rows)

        @pl.loop(0, chunks)
        def _(d):
            chunk = number_ref[2 + d]
            span = pl.ds(pl.multiple_of(d * rows, rows), rows)
            first = 0
            for k, cols in enumerate(sizes):
                lanes = slice(first, first + cols)
                for g in range(count // chunks):
                    left_ref[:, g * share : (g + 1) * share] = block_refs[k][g * chunks + chunk, 0]
                image = dot(left_ref[...], own_ref[:, lanes]).astype(BF16)
                for pick, target in ((core, mine_ref), (1 - core, theirs_ref)):
                    right = right_refs[k][:, pl.ds(pl.multiple_of(pick * cols, cols), cols)]
                    target[span, lanes] = dot(image, right.astype(BF16)).astype(target.dtype)
                    start = pl.multiple_of(chunk * rows + pick * share, share)
                    left = dot_nt(own_ref[near, lanes], own_ref[pl.ds(start, share), lanes])
                    low = total + k * share
                    target[span, low : low + share] = left.astype(target.dtype)
                first += cols

    shape = (width, total + used * share)
    return pl.pallas_call(
        body,
        grid=(1,),
        out_shape=(jax.ShapeDtypeStruct(shape, F32), jax.ShapeDtypeStruct(shape, BF16)),
        in_specs=[pl.BlockSpec(memory_space=pltpu.SMEM), whole(own)]
        + [
            pl.BlockSpec((count, 1, rows, share), lambda step, which=which: (0, which, 0, 0))
            for which, _ in parts
        ]
        + [whole(root) for _, root in parts],
        out_specs=(pl.BlockSpec(shape, lambda step: (0, 0)),) * 2,
        scratch_shapes=[pltpu.VMEM((rows, width), BF16)],
        compiler_params=pltpu.CompilerParams(vmem_limit_bytes=40 << 20),
        name="column_terms",
    )(numbers, own, *[blocks] * used, *[root for _, root in parts])


def row_kernel(own, blocks, which, left_root, numbers):
    width, count = own.shape
    devices, _, rows, share = blocks.shape
    chunks = width // rows
    tall = left_root.shape[0]
    piece = tall + 2 * share

    def body(number_ref, own_ref, block_ref, left_ref, mine_ref, theirs_ref, right_ref):
        core, depth = number_ref[0], number_ref[1]
        targets = ((core, mine_ref), (1 - core, theirs_ref))
        near = own_ref[pl.ds(pl.multiple_of(depth * rows, rows), rows), :]
        for d in range(chunks):
            chunk = number_ref[2 + d]
            for k, (pick, target) in enumerate(targets):
                part = pl.ds(pl.multiple_of(pick * share, share), share)
                lanes = slice((k * chunks + d) * share, (k * chunks + d + 1) * share)
                for g in range(devices // chunks):
                    right_ref[g * share : (g + 1) * share, lanes] = block_ref[
                        g * chunks + chunk, 0, part, :
                    ]
                start = pl.multiple_of(chunk * rows + pick * share, share)
                right = dot_nt(own_ref[pl.ds(start, share), :], near).astype(target.dtype)
                low = d * piece + tall
                target[low : low + share, :] = right[:, :share]
                target[low + share : low + 2 * share, :] = right[:, share:]
        for first in range(0, tall, rows):
            image = dot_nt(left_ref[first : first + rows, :].astype(BF16), own_ref[...])
            ahead = dot(image.astype(BF16), right_ref[...])
            for k, (_, target) in enumerate(targets):
                for d in range(chunks):
                    lanes = slice((k * chunks + d) * share, (k * chunks + d + 1) * share)
                    low = d * piece + first
                    target[low : low + rows, :] = ahead[:, lanes].astype(target.dtype)

    shape = (chunks * piece, share)
    return pl.pallas_call(
        body,
        grid=(1,),
        out_shape=(jax.ShapeDtypeStruct(shape, F32), jax.ShapeDtypeStruct(shape, BF16)),
        in_specs=[
            pl.BlockSpec(memory_space=pltpu.SMEM),
            whole(own),
            pl.BlockSpec((devices, 1, rows, share), lambda step: (0, which, 0, 0)),
            whole(left_root),
        ],
        out_specs=(pl.BlockSpec(shape, lambda step: (0, 0)),) * 2,
        scratch_shapes=[pltpu.VMEM((width, width), BF16)],
        compiler_params=pltpu.CompilerParams(vmem_limit_bytes=40 << 20),
        name="row_terms",
    )(numbers, own, blocks, left_root)


class Place:
    def __init__(self):
        self.rows = lax.axis_size("y")
        self.plane = self.rows * lax.axis_size("x")
        self.depth = lax.axis_size("in")
        self.q = lax.axis_index("y") * lax.axis_size("x") + lax.axis_index("x")
        self.c = lax.axis_index("c")
        self.z = lax.axis_index("in")
        self.last = {}

    def send(self, values, axes, pairs, lane=None):
        if lane in self.last:
            values, _ = lax.optimization_barrier((values, self.last[lane]))
        values = [lax.ppermute(value, axes, pair) for value, pair in zip(values, pairs)]
        if lane is not None:
            self.last[lane] = values
        return values

    def after(self, value, *earlier):
        return lax.optimization_barrier((value, *earlier))[0]

    def all_after(self, values, *earlier):
        return lax.optimization_barrier((tuple(values), *earlier))[0]

    def swap_core(self, value):
        return self.send([value], "c", [[(0, 1), (1, 0)]])[0]

    def swap_plane(self, values, distances, lane="plane"):
        pairs = [[(k, k ^ d) for k in range(self.plane)] for d in distances]
        return self.send(values, PLANE, pairs, lane)

    def on_depth(self, value):
        if "depth" in self.last:
            value, _ = lax.optimization_barrier((value, self.last["depth"]))
        value = lax.all_to_all(value, "in", 0, 0, tiled=True)
        self.last["depth"] = value
        return value

    def on_chips(self, values, targets, lane):
        pairs = []
        for target in targets:
            found = [
                (q, z, target(q, z))
                for q in range(self.plane)
                for z in range(self.depth)
                if target(q, z) is not None
            ]
            pairs.append([(q * self.depth + z, t[0] * self.depth + t[1]) for q, z, t in found])
        return self.send(values, CHIPS, pairs, lane)

    def by_core(self, own, other):
        return jnp.where(self.c == 0, own, other), jnp.where(self.c == 0, other, own)

    def mine(self, pair):
        return jnp.where(self.c == 0, pair[0], pair[1])

    def theirs(self, pair):
        return jnp.where(self.c == 0, pair[1], pair[0])

    def shuffle(self, values, index):
        values = list(values)
        bit = 1
        while bit < len(values):
            on = (index // bit) % 2 == 1
            values = [jnp.where(on, values[k ^ bit], values[k]) for k in range(len(values))]
            bit *= 2
        return values

    def gather_depth(self, value):
        return self.on_depth(jnp.broadcast_to(value[None], (self.depth,) + value.shape))

    def transpose_chips(self, value, lane):
        return self.on_chips([value], [lambda q, z: (z, q)], lane)[0]

    def spread_plane(self, value):
        q, z = self.q, self.z
        if self.plane != 4:
            total = jnp.where(q == z, value, jnp.zeros_like(value))
            targets = [
                lambda a, b, d=d: (a ^ d, b) if a == b else None for d in range(1, self.plane)
            ]
            for part in self.on_chips([value] * len(targets), targets, "plane"):
                total = total + part
            return total
        half = value.shape[0] // 2
        low, high = value[:half], value[half:]
        low_x, high_y = self.on_chips(
            [low, high],
            [
                lambda a, b: (a ^ 1, b) if a == b else None,
                lambda a, b: (a ^ 2, b) if a == b else None,
            ],
            "plane",
        )
        high_x, low_y = self.on_chips(
            [jnp.where(q == z, high, high_y), jnp.where(q == z, low, low_x)],
            [
                lambda a, b: (a ^ 1, b) if a ^ b in (0, 2) else None,
                lambda a, b: (a ^ 2, b) if a ^ b in (0, 1) else None,
            ],
            "plane",
        )
        apart = q ^ z
        low = jnp.where(apart == 0, low, jnp.where(apart == 1, low_x, low_y))
        high = jnp.where(apart == 0, high, jnp.where(apart == 2, high_y, high_x))
        return jnp.concatenate([low, high])

    def gather_tokens(self, value):
        mine = self.gather_plane(value)
        return join(mine + [self.swap_core(part) for part in mine])

    def reduce_tokens(self, mine, theirs):
        total = mine + self.swap_core(theirs.astype(BF16)).astype(F32)
        return self.reduce_plane(jnp.split(total, self.plane))

    def by_two_steps(self, shape):
        return self.plane == 4 and math.prod(shape) > 200_000

    def gather_plane(self, value):
        if not self.by_two_steps(value.shape):
            others = range(1, self.plane)
            return [value] + self.swap_plane([value] * len(others), others)
        half = value.shape[0] // 2
        by_x, by_y = self.swap_plane([value, value], (1, 2))
        first, second = self.swap_plane([by_y[:half], by_x[half:]], (1, 2))
        return [value, by_x, by_y, jnp.concatenate([first, second])]

    def reduce_plane(self, values):
        total = values[0]
        others = [value.astype(BF16) for value in values[1:]]
        for part in self.swap_plane(others, range(1, self.plane)):
            total = total + part.astype(F32)
        return total

    def reduce_plane_late(self, far, rest):
        if self.plane != 4:
            return self.reduce_plane([*rest(), far])
        half = far.shape[0] // 2
        first, second = self.swap_plane([far[:half], far[half:]], (1, 2))
        own, to_x, to_y = rest()
        to_y = jnp.concatenate([to_y[:half] + first.astype(F32), to_y[half:]])
        to_x = jnp.concatenate([to_x[:half], to_x[half:] + second.astype(F32)])
        by_x, by_y = self.swap_plane([to_x.astype(BF16), to_y.astype(BF16)], (1, 2))
        return own + by_x.astype(F32) + by_y.astype(F32)


def norm_parts(values):
    centred = values - jnp.mean(values, axis=-1, keepdims=True)
    spread = lax.rsqrt(jnp.mean(centred * centred, axis=-1, keepdims=True) + EPSILON)
    return centred * spread, spread


def norm_backward(grad, scaled, spread, gain):
    inner = grad * gain
    mean_one = jnp.mean(inner, axis=-1, keepdims=True)
    mean_two = jnp.mean(inner * scaled, axis=-1, keepdims=True)
    return spread * (inner - mean_one - scaled * mean_two)


def gelu(values):
    return 0.5 * values * (1.0 + jnp.tanh(ROOT_TWO_PI * (values + 0.044715 * values**3)))


def gelu_slope(values):
    squared = values * values
    bent = jnp.tanh(ROOT_TWO_PI * (values + 0.044715 * squared * values))
    return 0.5 * (1.0 + bent) + 0.5 * values * (1.0 - bent * bent) * (
        ROOT_TWO_PI * (1.0 + 3.0 * 0.044715 * squared)
    )


def on_device(
    tokens,
    segments,
    cotangent,
    vectors,
    vector_moment,
    qkv_weight,
    qkv_moment,
    qkv_left,
    qkv_right,
    qkv_left_root,
    qkv_right_root,
    out_weight,
    out_moment,
    out_left,
    out_right,
    out_left_root,
    out_right_root,
    fc_weight,
    fc_moment,
    fc_left,
    fc_right,
    fc_left_root,
    fc_right_root,
    proj_weight,
    proj_moment,
    proj_left,
    proj_right,
    proj_left_root,
    proj_right_root,
):
    here = Place()
    plane, depth = here.plane, here.depth
    length, width = tokens.shape
    z, q, c = here.z, here.q, here.c
    block = 2 * HEAD_DIM if qkv_weight.shape[1] % (2 * HEAD_DIM) == 0 else HEAD_DIM

    def far_columns(own):
        far = here.spread_plane(own)
        return here.by_core(far, here.swap_core(far))

    def pair_columns(share):
        return jnp.concatenate(here.by_core(share, here.swap_core(share)), axis=1)

    def by_parity(pair):
        parts = jnp.split(pair, pair.shape[1] // block, axis=1)
        return jnp.concatenate([here.mine(parts[k : k + 2]) for k in range(0, len(parts), 2)], axis=1)

    qkv_share = by_parity(pair_columns(qkv_weight.astype(BF16)))
    fc_share = fc_weight.astype(BF16)
    proj_split = proj_weight.astype(BF16).reshape(2, -1, proj_weight.shape[1])
    proj_share = jnp.concatenate(
        here.by_core(here.mine(proj_split), here.swap_core(here.theirs(proj_split))), axis=1
    )
    out_split = out_weight.astype(BF16).reshape(-1, 2, block, out_weight.shape[1])
    out_split = (
        out_split[:, 0].reshape(-1, out_weight.shape[1]),
        out_split[:, 1].reshape(-1, out_weight.shape[1]),
    )
    out_share = jnp.concatenate(
        here.by_core(here.mine(out_split), here.swap_core(here.theirs(out_split))), axis=1
    )

    proj_turned = here.transpose_chips(proj_share.T, "plane")
    qkv_parts = here.gather_plane(here.gather_depth(qkv_share).reshape(width, -1))
    plane_cotangent = here.gather_tokens(cotangent)
    fc_full = here.gather_depth(fc_share).reshape(width, -1)
    small_share = jnp.concatenate(
        [out_share, vectors.astype(BF16).reshape(-1, out_share.shape[1])]
    )
    small_whole = here.gather_depth(small_share)
    vector_whole = small_whole[:, out_share.shape[0] :].reshape(-1)
    out_rows = small_whole[:, : out_share.shape[0]].reshape(-1, out_share.shape[1])
    out_full = jnp.concatenate(here.shuffle(here.gather_plane(out_rows), q), axis=1)
    proj_full = here.gather_depth(proj_turned).reshape(width, -1)

    numbers = jnp.stack([c, z] + [q ^ d for d in range(plane)]).astype(jnp.int32)

    params = vector_whole.astype(F32)
    unit = fc_weight.shape[1]
    hidden = unit * 2 * plane
    gain_one, shift_one, bias_query, bias_value, bias_out, gain_two, shift_two = (
        params[k * width : (k + 1) * width] for k in range(7)
    )
    bias_fc = lax.dynamic_slice_in_dim(params, 7 * width + (2 * q + c) * unit, unit)
    bias_proj = params[7 * width + hidden :]

    pair_tokens = jnp.concatenate([tokens, here.swap_core(tokens)])
    labels = jnp.concatenate([segments, here.swap_core(segments)])
    position = jnp.arange(length)
    allowed = (labels[:, :, None] == labels[:, None, :]) & (position[:, None] >= position[None, :])
    mask = jnp.where(allowed, 0.0, MASKED).astype(F32)

    inputs = pair_tokens.astype(F32)
    scaled_one, spread_one = norm_parts(inputs)
    normed_one = (scaled_one * gain_one + shift_one).astype(BF16)
    normed_one = here.after(normed_one, fc_full)
    qkv_bias = jnp.concatenate([bias_query, jnp.zeros_like(bias_query), bias_value])
    qkv_bias = qkv_bias.reshape(-1, 2, block)
    qkv_bias = here.mine((qkv_bias[:, 0], qkv_bias[:, 1])).reshape(-1)
    projected = jnp.concatenate(
        here.shuffle([dot(normed_one, part) for part in qkv_parts], q), axis=1
    )
    projected = (projected + qkv_bias).astype(BF16)
    share_rows, share_cols = qkv_left_root.shape
    right_root = proj_right_root.astype(BF16)
    root_blocks = lax.all_gather(
        here.after(
            jnp.stack(
                [root.astype(BF16) for root in (qkv_left_root, out_left_root, fc_left_root)]
                + [jnp.concatenate([right_root[:, :share_cols], right_root[:, share_cols:]])]
            ),
            projected,
        ),
        ALL,
    )
    attended = attention_forward(projected, mask)
    attended = here.after(attended, plane_cotangent, proj_full)
    branch = dot(attended[:length], out_full) + here.swap_core(dot(attended[length:], out_full))
    middle = inputs[:length] + (branch + bias_out)
    scaled_two, spread_two = norm_parts(middle)
    normed_two = here.gather_tokens((scaled_two * gain_two + shift_two).astype(BF16))
    pre_act = dot(normed_two, fc_full) + bias_fc
    activated = gelu(pre_act).astype(BF16)

    token_total = length * 2 * plane * depth
    factor = 1.0 / math.sqrt(token_total)
    half = plane * length
    proj_terms = dot_tn(plane_cotangent, activated)
    late_cotangent = here.after(plane_cotangent, proj_terms)
    grad_pre = (dot(late_cotangent, proj_full) * gelu_slope(pre_act)).astype(BF16)
    two_mine, two_theirs = dot_nt(grad_pre[:half], fc_full), dot_nt(grad_pre[half:], fc_full)
    grad_normed_two = here.reduce_tokens(two_mine, two_theirs)
    fc_terms = dot_tn(here.after(normed_two, two_mine, two_theirs), grad_pre)
    rows_own = qkv_weight.shape[0]
    forward_parts = here.on_depth(
        jnp.concatenate(
            [
                proj_terms.reshape(depth, rows_own, unit).astype(BF16),
                fc_terms.reshape(depth, rows_own, unit).astype(BF16),
            ],
            axis=1,
        )
    )

    grad_top = cotangent.astype(F32)
    grad_middle = grad_top + norm_backward(grad_normed_two, scaled_two, spread_two, gain_two)
    own_branch = grad_middle.astype(BF16)
    grad_branch = jnp.concatenate([own_branch, here.swap_core(own_branch)])

    def total(parts):
        return jnp.sum(parts.astype(F32), axis=0) * factor

    forward_sum = total(here.after(forward_parts, own_branch))
    proj_sum, fc_grad = forward_sum[:rows_own], forward_sum[rows_own:]
    fc_own = here.gather_depth(fc_grad.astype(BF16)).reshape(width, -1)

    grad_attended = dot_nt(grad_branch, out_full).astype(BF16)
    grad_heads = attention_backward(projected, mask, grad_attended)

    qkv_cols = qkv_weight.shape[1]
    out_cols = out_weight.shape[1]
    aligned = out_cols % 128 == 0
    head_blocks = here.shuffle(jnp.split(grad_heads, plane, axis=1), q)

    def first_terms(distances, dtype):
        if aligned:
            return first_kernel(
                normed_one, grad_heads, attended, grad_branch, numbers, distances, dtype
            )
        found = []
        for d in distances:
            block = lax.dynamic_slice_in_dim(grad_branch, (q ^ d) * 2 * out_cols, 2 * out_cols, 1)
            term = dot_tn(attended, block).reshape(depth, -1, 2 * out_cols)
            term = jnp.concatenate([term[:, :, :out_cols], term[:, :, out_cols:]], axis=1)
            term = term.reshape(width, out_cols)
            head = dot_tn(normed_one, head_blocks[d])
            found.append(jnp.concatenate([head, term], axis=1).astype(dtype))
        return found

    def second_terms():
        own, *rest = first_terms(tuple(range(plane - 1)), F32)
        return own, *here.all_after(rest, fc_grad)

    first_parts_ready = here.reduce_plane_late(
        first_terms((plane - 1,), BF16)[0], second_terms
    ).astype(BF16)
    first_parts = here.on_depth(first_parts_ready.reshape(depth, -1, qkv_cols + out_cols))

    other_one = sum(dot_nt(part[length:], rows) for part, rows in zip(head_blocks, qkv_parts))
    grad_normed_one = sum(dot_nt(part[:length], rows) for part, rows in zip(head_blocks, qkv_parts))
    grad_normed_one = grad_normed_one + here.swap_core(other_one)
    own_scaled = scaled_one[:length]
    grad_in = norm_backward(grad_normed_one, own_scaled, spread_one[:length], gain_one)
    input_grad = (grad_middle + grad_in).astype(BF16)

    def sum_over_group(mine, theirs):
        return here.reduce_plane(jnp.split(mine + here.swap_core(theirs).astype(F32), plane))

    def column_terms(own, parts):
        if aligned:
            return column_kernel(own, root_blocks, parts, numbers)
        first, found = 0, []
        for which, right_root in parts:
            cols = right_root.shape[0]
            piece = own[:, first : first + cols]
            first += cols
            blocks = root_blocks.reshape(2 * plane, depth, 4, share_rows, share_cols)[:, :, which]
            left_root = blocks.transpose(1, 2, 0, 3).reshape(depth, share_rows, width)
            left_root = jnp.concatenate(here.shuffle(list(left_root), q))
            image = dot(left_root, piece).astype(BF16)
            right_halves = jnp.split(right_root.astype(BF16), 2, axis=1)
            left = dot_nt(lax.dynamic_slice_in_dim(piece, z * rows_own, rows_own), piece)
            left = here.shuffle(jnp.split(left, plane, axis=1), q)
            left = jnp.split(jnp.concatenate(left), 2, axis=1)
            found.append(
                [(dot(image, pick(right_halves)), pick(left)) for pick in (here.mine, here.theirs)]
            )
        mine, theirs = (
            jnp.concatenate([one[k][0] for one in found] + [one[k][1] for one in found], axis=1)
            for k in range(2)
        )
        return mine, theirs.astype(BF16)

    def row_terms(own, which, left_root):
        if aligned:
            return row_kernel(own, root_blocks, which, left_root, numbers)
        blocks = root_blocks.reshape(2 * plane, depth, 4, 2, share_rows // 2, share_cols)[:, :, which]
        chunk = width // depth
        right = dot_nt(own, lax.dynamic_slice_in_dim(own, z * chunk, chunk))
        right = here.shuffle(jnp.split(right, plane), q)
        image = dot_nt(left_root.astype(BF16), own).astype(BF16)
        found = []
        for pick in (here.mine, here.theirs):
            root = pick((blocks[:, :, 0], blocks[:, :, 1]))
            root = [root[:, r].reshape(width, share_cols) for r in range(depth)]
            root = jnp.concatenate(here.shuffle(root, q), axis=1)
            ahead = jnp.split(dot(image, root), plane, axis=1)
            stats = [
                jnp.concatenate(jnp.split(pick(jnp.split(pair, 2)), 2, axis=1)) for pair in right
            ]
            found.append(
                jnp.concatenate([jnp.concatenate(parts) for parts in zip(ahead, stats)])
            )
        return found[0], found[1].astype(BF16)

    fc_mine, fc_theirs = column_terms(fc_own, [(2, fc_right_root)])
    fc_other = here.swap_core(fc_theirs)
    fc_total = here.reduce_plane(jnp.split(fc_mine + fc_other.astype(F32), plane))
    first_sum = total(here.after(first_parts, fc_total))

    qkv_parity = first_sum[:, :qkv_cols]
    qkv_other = here.swap_core(qkv_parity)
    qkv_pair = []
    for k in range(0, qkv_cols, block):
        qkv_pair += here.by_core(qkv_parity[:, k : k + block], qkv_other[:, k : k + block])
    half_count = len(qkv_pair) // 2
    qkv_grad = jnp.concatenate(
        [here.mine((qkv_pair[k], qkv_pair[k + half_count])) for k in range(half_count)], axis=1
    )
    out_halves = jnp.split(first_sum[:, qkv_cols:], 2)
    out_pair = here.by_core(here.mine(out_halves), here.swap_core(here.theirs(out_halves)))
    out_grad = jnp.stack(
        [part.reshape(-1, block, out_cols) for part in out_pair], axis=1
    ).reshape(out_weight.shape)
    first_low = jnp.concatenate([qkv_grad, out_grad], axis=1).astype(BF16)
    first_own = here.gather_depth(first_low).reshape(width, -1)

    fc_far = far_columns(here.after(fc_own, first_low))

    late_activated = here.after(activated, first_low)
    output = here.reduce_tokens(
        dot_nt(late_activated[:half], proj_full), dot_nt(late_activated[half:], proj_full)
    )
    output = (middle + (output + bias_proj)).astype(BF16)

    unit_cols = fc_weight.shape[1]
    fc_direction = here.transpose_chips(fc_total[:, :unit_cols].astype(BF16), "plane").astype(F32)

    first_total = sum_over_group(
        *column_terms(first_own, [(0, qkv_right_root), (1, out_right_root)])
    )

    proj_own = here.gather_depth(proj_sum.astype(BF16)).reshape(width, -1)
    first_far = far_columns(first_own)
    proj_total = sum_over_group(*row_terms(proj_own, 3, proj_left_root))
    proj_far = far_columns(proj_own)
    own_cols = proj_weight.shape[1]
    proj_grad = jnp.concatenate(
        [
            lax.dynamic_slice_in_dim(part, (2 * q + c) * own_cols, own_cols).T
            for part in proj_far
        ]
    ).astype(F32)
    proj_left_sum = dot_tn(jnp.concatenate(proj_far, axis=1), proj_own)

    def interleave(value):
        value = value.reshape(-1, 1, block)
        zeros = jnp.zeros_like(value)
        return jnp.concatenate(here.by_core(value, zeros), axis=1).reshape(-1)

    head_sums = interleave(jnp.sum(grad_heads.astype(F32), axis=0))
    fc_bias_terms = lax.dynamic_update_slice_in_dim(
        jnp.zeros((hidden,), F32), jnp.sum(grad_pre.astype(F32), axis=0), (2 * q + c) * unit, 0
    )
    vector_terms = jnp.concatenate(
        [
            jnp.sum(grad_normed_one * own_scaled, axis=0),
            jnp.sum(grad_normed_one, axis=0),
            head_sums[:width],
            head_sums[2 * width :],
            jnp.sum(own_branch.astype(F32), axis=0),
            jnp.sum(grad_normed_two * scaled_two, axis=0),
            jnp.sum(grad_normed_two, axis=0),
            fc_bias_terms,
            jnp.sum(grad_top, axis=0),
        ]
    )
    vector_sum = here.swap_core(vector_terms) + vector_terms
    vector_sum = vector_sum.reshape(depth, -1, 128)
    steps = range(1, depth)
    vector_parts = here.send(
        [lax.dynamic_index_in_dim(vector_sum, (z + k) % depth, 0, False) for k in steps],
        "in",
        [[(n, (n + k) % depth) for n in range(depth)] for k in steps],
    )
    vector_sum = sum(vector_parts, lax.dynamic_index_in_dim(vector_sum, z, 0, False))
    distance = 1
    while distance < plane:
        vector_sum = vector_sum + here.swap_plane([vector_sum], [distance], None)[0]
        distance *= 2
    vector_grad = vector_sum.reshape(-1) * factor

    cut = qkv_cols + out_cols
    first_direction = here.transpose_chips(first_total[:, :cut].astype(BF16), "turn").astype(F32)
    qkv_direction, out_direction = first_direction[:, :qkv_cols], first_direction[:, qkv_cols:]
    qkv_left_sum = first_total[:, cut : cut + out_cols]
    out_left_sum = first_total[:, cut + out_cols :]
    fc_left_sum = fc_total[:, unit_cols:]
    proj_direction = proj_total[: proj_weight.shape[0]]
    proj_right_sum = jnp.concatenate(jnp.split(proj_total[proj_weight.shape[0] :], 2), axis=1)

    fc_right_sum = dot_tn(fc_own, jnp.concatenate(fc_far, axis=1))
    qkv_right_sum = dot_tn(
        first_own[:, :qkv_cols], jnp.concatenate([part[:, :qkv_cols] for part in first_far], axis=1)
    )
    out_right_sum = dot_tn(
        first_own[:, qkv_cols:], jnp.concatenate([part[:, qkv_cols:] for part in first_far], axis=1)
    )

    results = []
    for grad, weight, moment, left, right, found, row_total, col_total in (
        (
            qkv_grad,
            qkv_weight,
            qkv_moment,
            qkv_left,
            qkv_right,
            (qkv_left_sum, qkv_right_sum, qkv_direction),
            width,
            3 * width,
        ),
        (
            out_grad,
            out_weight,
            out_moment,
            out_left,
            out_right,
            (out_left_sum, out_right_sum, out_direction),
            width,
            width,
        ),
        (
            fc_grad,
            fc_weight,
            fc_moment,
            fc_left,
            fc_right,
            (fc_left_sum, fc_right_sum, fc_direction),
            width,
            hidden,
        ),
        (
            proj_grad,
            proj_weight,
            proj_moment,
            proj_left,
            proj_right,
            (proj_left_sum, proj_right_sum, proj_direction),
            hidden,
            width,
        ),
    ):
        left_sum, right_sum, direction = found
        new_moment = MOMENTUM * moment + direction
        new_weight = weight - RATE * new_moment
        results += [
            grad,
            DECAY * left + (1.0 - DECAY) / col_total * left_sum,
            DECAY * right + (1.0 - DECAY) / row_total * right_sum,
            new_moment,
            new_weight,
            new_weight.astype(BF16),
        ]
    new_vector_moment = MOMENTUM * vector_moment + vector_grad
    new_vectors = vectors - RATE * new_vector_moment
    return (output, input_grad, *results, vector_grad, new_vector_moment, new_vectors)


def solution(mesh):
    groups, depth = mesh.shape["grp"], mesh.shape["in"]
    fine = Mesh(mesh.devices.reshape(groups // 4, 2, 2, depth), ALL)
    grp = ("y", "x", "c")
    tokens, cols, rows, flat = P(ALL, None), P("in", grp), P(grp, "in"), P("in")
    matrix_in = (cols, cols, cols, rows, cols, rows)
    matrix_out = (cols, cols, rows, cols, cols, cols)
    return jax.shard_map(
        on_device,
        mesh=fine,
        in_specs=(tokens, tokens, tokens, flat, flat) + matrix_in * 4,
        out_specs=(tokens, tokens) + matrix_out * 4 + (flat, flat, flat),
        check_vma=False,
    )
```

```python
import math

import jax
import jax.numpy as jnp
import numpy as np
from jax import lax
from jax.experimental import pallas as pl
from jax.experimental.pallas import tpu as pltpu
from jax.sharding import Mesh
from jax.sharding import PartitionSpec as P

HEADS = 16
HEAD_DIM = 64
EPSILON = 1e-05
DECAY = 0.5
MOMENTUM = 0.5
RATE = 0.03
MASKED = -1e30
ROOT_TWO_PI = math.sqrt(2.0 / math.pi)
BF16 = jnp.bfloat16
F32 = jnp.float32
PLANE = ("y", "x")
CHIPS = ("y", "x", "in")
ALL = ("y", "x", "c", "in")


def dot(left, right):
    return jnp.dot(left, right, preferred_element_type=F32)


def dot_tn(left, right):
    return lax.dot_general(left, right, (((0,), (0,)), ((), ())), preferred_element_type=F32)


def dot_nt(left, right):
    return lax.dot_general(left, right, (((1,), (1,)), ((), ())), preferred_element_type=F32)


def lane_half(shape, half):
    return (lax.broadcasted_iota(jnp.int32, shape, 1) // HEAD_DIM) == half


def softmax_rows(scores):
    shifted = jnp.exp(scores - jnp.max(scores, axis=-1, keepdims=True))
    return shifted / jnp.sum(shifted, axis=-1, keepdims=True)


def attention_forward(qkv, bias):
    sequences, length, _ = bias.shape
    width = qkv.shape[1] // 3
    pair = 2 * HEAD_DIM
    scale = HEAD_DIM ** (-0.5)

    def body(qkv_ref, bias_ref, out_ref):
        for seq in range(sequences):
            rows = slice(seq * length, (seq + 1) * length)
            mask = bias_ref[seq]
            for col in range(0, width, pair):
                queries = qkv_ref[rows, col : col + pair]
                key_rows = qkv_ref[rows, width + col : width + col + pair]
                value_rows = qkv_ref[rows, 2 * width + col : 2 * width + col + pair]
                parts = []
                for half in range(2):
                    own = jnp.where(lane_half(queries.shape, half), queries, jnp.zeros_like(queries))
                    probs = softmax_rows(dot_nt(own, key_rows) * scale + mask)
                    parts.append(dot(probs.astype(BF16), value_rows))
                picked = jnp.where(lane_half(parts[0].shape, 0), parts[0], parts[1])
                out_ref[rows, col : col + pair] = picked.astype(BF16)

    return pl.pallas_call(
        body,
        out_shape=jax.ShapeDtypeStruct((qkv.shape[0], width), BF16),
        in_specs=[pl.BlockSpec(memory_space=pltpu.VMEM)] * 2,
        out_specs=pl.BlockSpec(memory_space=pltpu.VMEM),
        name="attention_forward",
    )(qkv, bias)


def attention_backward(qkv, bias, grad):
    sequences, length, _ = bias.shape
    width = qkv.shape[1] // 3
    pair = 2 * HEAD_DIM
    scale = HEAD_DIM ** (-0.5)

    def body(qkv_ref, bias_ref, grad_ref, out_ref):
        for seq in range(sequences):
            rows = slice(seq * length, (seq + 1) * length)
            mask = bias_ref[seq]
            for col in range(0, width, pair):
                queries = qkv_ref[rows, col : col + pair]
                key_rows = qkv_ref[rows, width + col : width + col + pair]
                value_rows = qkv_ref[rows, 2 * width + col : 2 * width + col + pair]
                grads = grad_ref[rows, col : col + pair]
                found = []
                for half in range(2):
                    lanes = lane_half(queries.shape, half)
                    own = jnp.where(lanes, queries, jnp.zeros_like(queries))
                    probs = softmax_rows(dot_nt(own, key_rows) * scale + mask)
                    own_grad = jnp.where(lanes, grads, jnp.zeros_like(grads))
                    grad_probs = dot_nt(own_grad, value_rows)
                    row_dot = jnp.sum(probs * grad_probs, axis=-1, keepdims=True)
                    grad_scores = (probs * (grad_probs - row_dot)).astype(BF16)
                    found.append(
                        (
                            dot(grad_scores, key_rows) * scale,
                            dot_tn(grad_scores, queries) * scale,
                            dot_tn(probs.astype(BF16), grads),
                        )
                    )
                low_lanes = lane_half((length, pair), 0)
                for third in range(3):
                    picked = jnp.where(low_lanes, found[0][third], found[1][third])
                    start = third * width + col
                    out_ref[rows, start : start + pair] = picked.astype(BF16)

    return pl.pallas_call(
        body,
        out_shape=jax.ShapeDtypeStruct(qkv.shape, BF16),
        in_specs=[pl.BlockSpec(memory_space=pltpu.VMEM)] * 3,
        out_specs=pl.BlockSpec(memory_space=pltpu.VMEM),
        name="attention_backward",
    )(qkv, bias, grad)


def whole(array):
    return pl.BlockSpec(array.shape, lambda step: (0,) * len(array.shape))


def join(pieces):
    rows, cols = pieces[0].shape

    def body(*refs):
        for k in range(len(pieces)):
            refs[-1][k * rows : (k + 1) * rows, :] = refs[k][...]

    in_vmem = pl.BlockSpec(memory_space=pltpu.VMEM)
    return pl.pallas_call(
        body,
        out_shape=jax.ShapeDtypeStruct((len(pieces) * rows, cols), pieces[0].dtype),
        in_specs=[in_vmem] * len(pieces),
        out_specs=in_vmem,
        name="join",
    )(*pieces)


def first_kernel(normed, heads, attended, branch, numbers, distances, dtype):
    width, chips = normed.shape[1], numbers.shape[0] - 2
    cols, pair = heads.shape[1] // chips, branch.shape[1] // chips
    rows, share = width // chips, pair // 2
    tall = attended.shape[1] // chips

    def body(number_ref, normed_ref, heads_ref, attended_ref, branch_ref, *targets):
        for d, target in zip(distances, targets):
            chip = number_ref[2 + d]
            head = heads_ref[:, pl.ds(pl.multiple_of(chip * cols, cols), cols)]
            target[:, :cols] = dot_tn(normed_ref[...], head).astype(dtype)
            term = branch_ref[:, pl.ds(pl.multiple_of(chip * pair, pair), pair)]
            term = dot_tn(attended_ref[...], term).astype(dtype)
            for k in range(chips):
                for half in range(2):
                    start = k * rows + half * tall
                    target[start : start + tall, cols:] = term[
                        k * tall : (k + 1) * tall, half * share : (half + 1) * share
                    ]

    in_vmem = pl.BlockSpec(memory_space=pltpu.VMEM)
    return pl.pallas_call(
        body,
        out_shape=[jax.ShapeDtypeStruct((width, cols + share), dtype)] * len(distances),
        in_specs=[pl.BlockSpec(memory_space=pltpu.SMEM)] + [in_vmem] * 4,
        out_specs=[in_vmem] * len(distances),
        name="first_terms",
    )(numbers, normed, heads, attended, branch)


def column_kernel(own, blocks, parts, numbers):
    width = own.shape[0]
    count, _, rows, share = blocks.shape
    chunks = width // rows
    sizes = [root.shape[0] for _, root in parts]
    total = sum(sizes)
    used = len(parts)

    def body(number_ref, own_ref, *refs):
        block_refs, right_refs = refs[:used], refs[used : 2 * used]
        mine_ref, theirs_ref, left_ref = refs[2 * used :]
        core, depth = number_ref[0], number_ref[1]
        near = pl.ds(pl.multiple_of(depth * rows, rows), rows)

        @pl.loop(0, chunks)
        def _(d):
            chunk = number_ref[2 + d]
            span = pl.ds(pl.multiple_of(d * rows, rows), rows)
            first = 0
            for k, cols in enumerate(sizes):
                lanes = slice(first, first + cols)
                for g in range(count // chunks):
                    left_ref[:, g * share : (g + 1) * share] = block_refs[k][g * chunks + chunk, 0]
                image = dot(left_ref[...], own_ref[:, lanes]).astype(BF16)
                for pick, target in ((core, mine_ref), (1 - core, theirs_ref)):
                    right = right_refs[k][:, pl.ds(pl.multiple_of(pick * cols, cols), cols)]
                    target[span, lanes] = dot(image, right.astype(BF16)).astype(target.dtype)
                    start = pl.multiple_of(chunk * rows + pick * share, share)
                    left = dot_nt(own_ref[near, lanes], own_ref[pl.ds(start, share), lanes])
                    low = total + k * share
                    target[span, low : low + share] = left.astype(target.dtype)
                first += cols

    shape = (width, total + used * share)
    return pl.pallas_call(
        body,
        grid=(1,),
        out_shape=(jax.ShapeDtypeStruct(shape, F32), jax.ShapeDtypeStruct(shape, BF16)),
        in_specs=[pl.BlockSpec(memory_space=pltpu.SMEM), whole(own)]
        + [
            pl.BlockSpec((count, 1, rows, share), lambda step, which=which: (0, which, 0, 0))
            for which, _ in parts
        ]
        + [whole(root) for _, root in parts],
        out_specs=(pl.BlockSpec(shape, lambda step: (0, 0)),) * 2,
        scratch_shapes=[pltpu.VMEM((rows, width), BF16)],
        compiler_params=pltpu.CompilerParams(vmem_limit_bytes=40 << 20),
        name="column_terms",
    )(numbers, own, *[blocks] * used, *[root for _, root in parts])


def row_kernel(own, blocks, which, left_root, numbers):
    width, count = own.shape
    devices, _, rows, share = blocks.shape
    chunks = width // rows
    tall = left_root.shape[0]
    piece = tall + 2 * share

    def body(number_ref, own_ref, block_ref, left_ref, mine_ref, theirs_ref, right_ref):
        core, depth = number_ref[0], number_ref[1]
        targets = ((core, mine_ref), (1 - core, theirs_ref))
        near = own_ref[pl.ds(pl.multiple_of(depth * rows, rows), rows), :]
        for d in range(chunks):
            chunk = number_ref[2 + d]
            for k, (pick, target) in enumerate(targets):
                part = pl.ds(pl.multiple_of(pick * share, share), share)
                lanes = slice((k * chunks + d) * share, (k * chunks + d + 1) * share)
                for g in range(devices // chunks):
                    right_ref[g * share : (g + 1) * share, lanes] = block_ref[
                        g * chunks + chunk, 0, part, :
                    ]
                start = pl.multiple_of(chunk * rows + pick * share, share)
                right = dot_nt(own_ref[pl.ds(start, share), :], near).astype(target.dtype)
                low = d * piece + tall
                target[low : low + share, :] = right[:, :share]
                target[low + share : low + 2 * share, :] = right[:, share:]
        for first in range(0, tall, rows):
            image = dot_nt(left_ref[first : first + rows, :].astype(BF16), own_ref[...])
            ahead = dot(image.astype(BF16), right_ref[...])
            for k, (_, target) in enumerate(targets):
                for d in range(chunks):
                    lanes = slice((k * chunks + d) * share, (k * chunks + d + 1) * share)
                    low = d * piece + first
                    target[low : low + rows, :] = ahead[:, lanes].astype(target.dtype)

    shape = (chunks * piece, share)
    return pl.pallas_call(
        body,
        grid=(1,),
        out_shape=(jax.ShapeDtypeStruct(shape, F32), jax.ShapeDtypeStruct(shape, BF16)),
        in_specs=[
            pl.BlockSpec(memory_space=pltpu.SMEM),
            whole(own),
            pl.BlockSpec((devices, 1, rows, share), lambda step: (0, which, 0, 0)),
            whole(left_root),
        ],
        out_specs=(pl.BlockSpec(shape, lambda step: (0, 0)),) * 2,
        scratch_shapes=[pltpu.VMEM((width, width), BF16)],
        compiler_params=pltpu.CompilerParams(vmem_limit_bytes=40 << 20),
        name="row_terms",
    )(numbers, own, blocks, left_root)


class Place:
    def __init__(self):
        self.rows = lax.axis_size("y")
        self.plane = self.rows * lax.axis_size("x")
        self.depth = lax.axis_size("in")
        self.q = lax.axis_index("y") * lax.axis_size("x") + lax.axis_index("x")
        self.c = lax.axis_index("c")
        self.z = lax.axis_index("in")
        self.last = {}

    def send(self, values, axes, pairs, lane=None):
        if lane in self.last:
            values, _ = lax.optimization_barrier((values, self.last[lane]))
        values = [lax.ppermute(value, axes, pair) for value, pair in zip(values, pairs)]
        if lane is not None:
            self.last[lane] = values
        return values

    def after(self, value, *earlier):
        return lax.optimization_barrier((value, *earlier))[0]

    def all_after(self, values, *earlier):
        return lax.optimization_barrier((tuple(values), *earlier))[0]

    def swap_core(self, value):
        return self.send([value], "c", [[(0, 1), (1, 0)]])[0]

    def swap_plane(self, values, distances, lane="plane"):
        pairs = [[(k, k ^ d) for k in range(self.plane)] for d in distances]
        return self.send(values, PLANE, pairs, lane)

    def on_depth(self, value):
        if "depth" in self.last:
            value, _ = lax.optimization_barrier((value, self.last["depth"]))
        value = lax.all_to_all(value, "in", 0, 0, tiled=True)
        self.last["depth"] = value
        return value

    def on_chips(self, values, targets, lane):
        pairs = []
        for target in targets:
            found = [
                (q, z, target(q, z))
                for q in range(self.plane)
                for z in range(self.depth)
                if target(q, z) is not None
            ]
            pairs.append([(q * self.depth + z, t[0] * self.depth + t[1]) for q, z, t in found])
        return self.send(values, CHIPS, pairs, lane)

    def by_core(self, own, other):
        return jnp.where(self.c == 0, own, other), jnp.where(self.c == 0, other, own)

    def mine(self, pair):
        return jnp.where(self.c == 0, pair[0], pair[1])

    def theirs(self, pair):
        return jnp.where(self.c == 0, pair[1], pair[0])

    def shuffle(self, values, index):
        values = list(values)
        bit = 1
        while bit < len(values):
            on = (index // bit) % 2 == 1
            values = [jnp.where(on, values[k ^ bit], values[k]) for k in range(len(values))]
            bit *= 2
        return values

    def gather_depth(self, value):
        return self.on_depth(jnp.broadcast_to(value[None], (self.depth,) + value.shape))

    def transpose_chips(self, value, lane):
        return self.on_chips([value], [lambda q, z: (z, q)], lane)[0]

    def spread_plane(self, value):
        q, z = self.q, self.z
        if self.plane != 4:
            total = jnp.where(q == z, value, jnp.zeros_like(value))
            targets = [
                lambda a, b, d=d: (a ^ d, b) if a == b else None for d in range(1, self.plane)
            ]
            for part in self.on_chips([value] * len(targets), targets, "plane"):
                total = total + part
            return total
        half = value.shape[0] // 2
        low, high = value[:half], value[half:]
        low_x, high_y = self.on_chips(
            [low, high],
            [
                lambda a, b: (a ^ 1, b) if a == b else None,
                lambda a, b: (a ^ 2, b) if a == b else None,
            ],
            "plane",
        )
        high_x, low_y = self.on_chips(
            [jnp.where(q == z, high, high_y), jnp.where(q == z, low, low_x)],
            [
                lambda a, b: (a ^ 1, b) if a ^ b in (0, 2) else None,
                lambda a, b: (a ^ 2, b) if a ^ b in (0, 1) else None,
            ],
            "plane",
        )
        apart = q ^ z
        low = jnp.where(apart == 0, low, jnp.where(apart == 1, low_x, low_y))
        high = jnp.where(apart == 0, high, jnp.where(apart == 2, high_y, high_x))
        return jnp.concatenate([low, high])

    def gather_tokens(self, value):
        return self.join_cores(self.gather_plane(value))

    def join_cores(self, mine):
        return join(mine + [self.swap_core(part) for part in mine])

    def reduce_tokens(self, mine, theirs):
        total = mine + self.swap_core(theirs.astype(BF16)).astype(F32)
        return self.reduce_plane(jnp.split(total, self.plane))

    def by_two_steps(self, shape):
        return self.plane == 4 and math.prod(shape) > 200_000

    def gather_plane(self, value):
        if not self.by_two_steps(value.shape):
            others = range(1, self.plane)
            return [value] + self.swap_plane([value] * len(others), others)
        half = value.shape[0] // 2
        by_x, by_y = self.swap_plane([value, value], (1, 2))
        first, second = self.swap_plane([by_y[:half], by_x[half:]], (1, 2))
        return [value, by_x, by_y, jnp.concatenate([first, second])]

    def reduce_plane(self, values):
        total = values[0]
        others = [value.astype(BF16) for value in values[1:]]
        for part in self.swap_plane(others, range(1, self.plane)):
            total = total + part.astype(F32)
        return total

    def reduce_plane_late(self, far, rest):
        if self.plane != 4:
            return self.reduce_plane([*rest(), far])
        half = far.shape[0] // 2
        first, second = self.swap_plane([far[:half], far[half:]], (1, 2))
        own, to_x, to_y = rest()
        to_y = jnp.concatenate([to_y[:half] + first.astype(F32), to_y[half:]])
        to_x = jnp.concatenate([to_x[:half], to_x[half:] + second.astype(F32)])
        by_x, by_y = self.swap_plane([to_x.astype(BF16), to_y.astype(BF16)], (1, 2))
        return own + by_x.astype(F32) + by_y.astype(F32)


def norm_parts(values):
    centred = values - jnp.mean(values, axis=-1, keepdims=True)
    spread = lax.rsqrt(jnp.mean(centred * centred, axis=-1, keepdims=True) + EPSILON)
    return centred * spread, spread


def norm_backward(grad, scaled, spread, gain):
    inner = grad * gain
    mean_one = jnp.mean(inner, axis=-1, keepdims=True)
    mean_two = jnp.mean(inner * scaled, axis=-1, keepdims=True)
    return spread * (inner - mean_one - scaled * mean_two)


def gelu(values):
    return 0.5 * values * (1.0 + jnp.tanh(ROOT_TWO_PI * (values + 0.044715 * values**3)))


def gelu_slope(values):
    squared = values * values
    bent = jnp.tanh(ROOT_TWO_PI * (values + 0.044715 * squared * values))
    return 0.5 * (1.0 + bent) + 0.5 * values * (1.0 - bent * bent) * (
        ROOT_TWO_PI * (1.0 + 3.0 * 0.044715 * squared)
    )


def on_device(
    tokens,
    segments,
    cotangent,
    vectors,
    vector_moment,
    qkv_weight,
    qkv_moment,
    qkv_left,
    qkv_right,
    qkv_left_root,
    qkv_right_root,
    out_weight,
    out_moment,
    out_left,
    out_right,
    out_left_root,
    out_right_root,
    fc_weight,
    fc_moment,
    fc_left,
    fc_right,
    fc_left_root,
    fc_right_root,
    proj_weight,
    proj_moment,
    proj_left,
    proj_right,
    proj_left_root,
    proj_right_root,
):
    here = Place()
    plane, depth = here.plane, here.depth
    length, width = tokens.shape
    z, q, c = here.z, here.q, here.c
    block = 2 * HEAD_DIM if qkv_weight.shape[1] % (2 * HEAD_DIM) == 0 else HEAD_DIM

    def far_columns(own):
        far = here.spread_plane(own)
        return here.by_core(far, here.swap_core(far))

    def pair_columns(share):
        return jnp.concatenate(here.by_core(share, here.swap_core(share)), axis=1)

    def by_parity(pair):
        parts = jnp.split(pair, pair.shape[1] // block, axis=1)
        return jnp.concatenate([here.mine(parts[k : k + 2]) for k in range(0, len(parts), 2)], axis=1)

    qkv_share = by_parity(pair_columns(qkv_weight.astype(BF16)))
    fc_share = fc_weight.astype(BF16)
    proj_split = proj_weight.astype(BF16).reshape(2, -1, proj_weight.shape[1])
    proj_share = jnp.concatenate(
        here.by_core(here.mine(proj_split), here.swap_core(here.theirs(proj_split))), axis=1
    )
    out_split = out_weight.astype(BF16).reshape(-1, 2, block, out_weight.shape[1])
    out_split = (
        out_split[:, 0].reshape(-1, out_weight.shape[1]),
        out_split[:, 1].reshape(-1, out_weight.shape[1]),
    )
    out_share = jnp.concatenate(
        here.by_core(here.mine(out_split), here.swap_core(here.theirs(out_split))), axis=1
    )

    cotangent_pieces = here.gather_plane(cotangent)
    proj_turned = here.transpose_chips(proj_share.T, None)
    qkv_rows = here.gather_depth(qkv_share).reshape(width, -1)
    qkv_parts = here.gather_plane(here.after(qkv_rows, proj_turned, *cotangent_pieces))
    fc_full = here.gather_depth(fc_share).reshape(width, -1)
    small_share = jnp.concatenate(
        [out_share, vectors.astype(BF16).reshape(-1, out_share.shape[1])]
    )
    small_whole = here.gather_depth(small_share)
    vector_whole = small_whole[:, out_share.shape[0] :].reshape(-1)
    out_rows = small_whole[:, : out_share.shape[0]].reshape(-1, out_share.shape[1])
    out_full = jnp.concatenate(here.shuffle(here.gather_plane(out_rows), q), axis=1)
    proj_full = here.gather_depth(proj_turned).reshape(width, -1)

    numbers = jnp.stack([c, z] + [q ^ d for d in range(plane)]).astype(jnp.int32)

    params = vector_whole.astype(F32)
    unit = fc_weight.shape[1]
    hidden = unit * 2 * plane
    gain_one, shift_one, bias_query, bias_value, bias_out, gain_two, shift_two = (
        params[k * width : (k + 1) * width] for k in range(7)
    )
    bias_fc = lax.dynamic_slice_in_dim(params, 7 * width + (2 * q + c) * unit, unit)
    bias_proj = params[7 * width + hidden :]

    pair_tokens = jnp.concatenate([tokens, here.swap_core(tokens)])
    labels = jnp.concatenate([segments, here.swap_core(segments)])
    position = jnp.arange(length)
    allowed = (labels[:, :, None] == labels[:, None, :]) & (position[:, None] >= position[None, :])
    mask = jnp.where(allowed, 0.0, MASKED).astype(F32)

    inputs = pair_tokens.astype(F32)
    scaled_one, spread_one = norm_parts(inputs)
    normed_one = (scaled_one * gain_one + shift_one).astype(BF16)
    normed_one = here.after(normed_one, fc_full)
    qkv_bias = jnp.concatenate([bias_query, jnp.zeros_like(bias_query), bias_value])
    qkv_bias = qkv_bias.reshape(-1, 2, block)
    qkv_bias = here.mine((qkv_bias[:, 0], qkv_bias[:, 1])).reshape(-1)
    projected = jnp.concatenate(
        here.shuffle([dot(normed_one, part) for part in qkv_parts], q), axis=1
    )
    projected = (projected + qkv_bias).astype(BF16)
    share_rows, share_cols = qkv_left_root.shape
    right_root = proj_right_root.astype(BF16)
    root_blocks = lax.all_gather(
        here.after(
            jnp.stack(
                [root.astype(BF16) for root in (qkv_left_root, out_left_root, fc_left_root)]
                + [jnp.concatenate([right_root[:, :share_cols], right_root[:, share_cols:]])]
            ),
            projected,
        ),
        ALL,
    )
    attended = attention_forward(projected, mask)
    attended = here.after(attended, proj_full)
    branch = dot(attended[:length], out_full) + here.swap_core(dot(attended[length:], out_full))
    middle = inputs[:length] + (branch + bias_out)
    scaled_two, spread_two = norm_parts(middle)
    plane_cotangent = here.join_cores(cotangent_pieces)
    normed_two = here.gather_tokens((scaled_two * gain_two + shift_two).astype(BF16))
    normed_two = here.after(normed_two, plane_cotangent)
    pre_act = dot(normed_two, fc_full) + bias_fc
    activated = gelu(pre_act).astype(BF16)

    token_total = length * 2 * plane * depth
    factor = 1.0 / math.sqrt(token_total)
    half = plane * length
    proj_terms = dot_tn(plane_cotangent, activated)
    late_cotangent = here.after(plane_cotangent, proj_terms)
    grad_pre = (dot(late_cotangent, proj_full) * gelu_slope(pre_act)).astype(BF16)
    two_mine, two_theirs = dot_nt(grad_pre[:half], fc_full), dot_nt(grad_pre[half:], fc_full)
    grad_normed_two = here.reduce_tokens(two_mine, two_theirs)
    fc_terms = dot_tn(here.after(normed_two, two_mine, two_theirs), grad_pre)
    rows_own = qkv_weight.shape[0]
    forward_parts = here.on_depth(
        jnp.concatenate(
            [
                proj_terms.reshape(depth, rows_own, unit).astype(BF16),
                fc_terms.reshape(depth, rows_own, unit).astype(BF16),
            ],
            axis=1,
        )
    )

    grad_top = cotangent.astype(F32)
    grad_middle = grad_top + norm_backward(grad_normed_two, scaled_two, spread_two, gain_two)
    own_branch = grad_middle.astype(BF16)
    grad_branch = jnp.concatenate([own_branch, here.swap_core(own_branch)])

    def total(parts):
        return jnp.sum(parts.astype(F32), axis=0) * factor

    forward_sum = total(here.after(forward_parts, own_branch))
    proj_sum, fc_grad = forward_sum[:rows_own], forward_sum[rows_own:]
    fc_own = here.gather_depth(fc_grad.astype(BF16)).reshape(width, -1)

    grad_attended = dot_nt(grad_branch, out_full).astype(BF16)
    grad_heads = attention_backward(projected, mask, grad_attended)

    qkv_cols = qkv_weight.shape[1]
    out_cols = out_weight.shape[1]
    aligned = out_cols % 128 == 0
    head_blocks = here.shuffle(jnp.split(grad_heads, plane, axis=1), q)

    def first_terms(distances, dtype):
        if aligned:
            return first_kernel(
                normed_one, grad_heads, attended, grad_branch, numbers, distances, dtype
            )
        found = []
        for d in distances:
            block = lax.dynamic_slice_in_dim(grad_branch, (q ^ d) * 2 * out_cols, 2 * out_cols, 1)
            term = dot_tn(attended, block).reshape(depth, -1, 2 * out_cols)
            term = jnp.concatenate([term[:, :, :out_cols], term[:, :, out_cols:]], axis=1)
            term = term.reshape(width, out_cols)
            head = dot_tn(normed_one, head_blocks[d])
            found.append(jnp.concatenate([head, term], axis=1).astype(dtype))
        return found

    def second_terms():
        own, *rest = first_terms(tuple(range(plane - 1)), F32)
        return own, *here.all_after(rest, fc_grad)

    first_parts_ready = here.reduce_plane_late(
        first_terms((plane - 1,), BF16)[0], second_terms
    ).astype(BF16)
    first_parts = here.on_depth(first_parts_ready.reshape(depth, -1, qkv_cols + out_cols))

    other_one = sum(dot_nt(part[length:], rows) for part, rows in zip(head_blocks, qkv_parts))
    grad_normed_one = sum(dot_nt(part[:length], rows) for part, rows in zip(head_blocks, qkv_parts))
    grad_normed_one = grad_normed_one + here.swap_core(other_one)
    own_scaled = scaled_one[:length]
    grad_in = norm_backward(grad_normed_one, own_scaled, spread_one[:length], gain_one)
    input_grad = (grad_middle + grad_in).astype(BF16)

    def sum_over_group(mine, theirs):
        return here.reduce_plane(jnp.split(mine + here.swap_core(theirs).astype(F32), plane))

    def column_terms(own, parts):
        if aligned:
            return column_kernel(own, root_blocks, parts, numbers)
        first, found = 0, []
        for which, right_root in parts:
            cols = right_root.shape[0]
            piece = own[:, first : first + cols]
            first += cols
            blocks = root_blocks.reshape(2 * plane, depth, 4, share_rows, share_cols)[:, :, which]
            left_root = blocks.transpose(1, 2, 0, 3).reshape(depth, share_rows, width)
            left_root = jnp.concatenate(here.shuffle(list(left_root), q))
            image = dot(left_root, piece).astype(BF16)
            right_halves = jnp.split(right_root.astype(BF16), 2, axis=1)
            left = dot_nt(lax.dynamic_slice_in_dim(piece, z * rows_own, rows_own), piece)
            left = here.shuffle(jnp.split(left, plane, axis=1), q)
            left = jnp.split(jnp.concatenate(left), 2, axis=1)
            found.append(
                [(dot(image, pick(right_halves)), pick(left)) for pick in (here.mine, here.theirs)]
            )
        mine, theirs = (
            jnp.concatenate([one[k][0] for one in found] + [one[k][1] for one in found], axis=1)
            for k in range(2)
        )
        return mine, theirs.astype(BF16)

    def row_terms(own, which, left_root):
        if aligned:
            return row_kernel(own, root_blocks, which, left_root, numbers)
        blocks = root_blocks.reshape(2 * plane, depth, 4, 2, share_rows // 2, share_cols)[:, :, which]
        chunk = width // depth
        right = dot_nt(own, lax.dynamic_slice_in_dim(own, z * chunk, chunk))
        right = here.shuffle(jnp.split(right, plane), q)
        image = dot_nt(left_root.astype(BF16), own).astype(BF16)
        found = []
        for pick in (here.mine, here.theirs):
            root = pick((blocks[:, :, 0], blocks[:, :, 1]))
            root = [root[:, r].reshape(width, share_cols) for r in range(depth)]
            root = jnp.concatenate(here.shuffle(root, q), axis=1)
            ahead = jnp.split(dot(image, root), plane, axis=1)
            stats = [
                jnp.concatenate(jnp.split(pick(jnp.split(pair, 2)), 2, axis=1)) for pair in right
            ]
            found.append(
                jnp.concatenate([jnp.concatenate(parts) for parts in zip(ahead, stats)])
            )
        return found[0], found[1].astype(BF16)

    fc_mine, fc_theirs = column_terms(fc_own, [(2, fc_right_root)])
    fc_other = here.swap_core(fc_theirs)
    fc_total = here.reduce_plane(jnp.split(fc_mine + fc_other.astype(F32), plane))
    first_sum = total(here.after(first_parts, fc_total))

    qkv_parity = first_sum[:, :qkv_cols]
    qkv_other = here.swap_core(qkv_parity)
    qkv_pair = []
    for k in range(0, qkv_cols, block):
        qkv_pair += here.by_core(qkv_parity[:, k : k + block], qkv_other[:, k : k + block])
    half_count = len(qkv_pair) // 2
    qkv_grad = jnp.concatenate(
        [here.mine((qkv_pair[k], qkv_pair[k + half_count])) for k in range(half_count)], axis=1
    )
    out_halves = jnp.split(first_sum[:, qkv_cols:], 2)
    out_pair = here.by_core(here.mine(out_halves), here.swap_core(here.theirs(out_halves)))
    out_grad = jnp.stack(
        [part.reshape(-1, block, out_cols) for part in out_pair], axis=1
    ).reshape(out_weight.shape)
    first_low = jnp.concatenate([qkv_grad, out_grad], axis=1).astype(BF16)
    first_own = here.gather_depth(first_low).reshape(width, -1)

    fc_far = far_columns(here.after(fc_own, first_low))

    late_activated = here.after(activated, first_low)
    output = here.reduce_tokens(
        dot_nt(late_activated[:half], proj_full), dot_nt(late_activated[half:], proj_full)
    )
    output = (middle + (output + bias_proj)).astype(BF16)

    unit_cols = fc_weight.shape[1]
    fc_direction = here.transpose_chips(fc_total[:, :unit_cols].astype(BF16), "plane").astype(F32)

    first_total = sum_over_group(
        *column_terms(first_own, [(0, qkv_right_root), (1, out_right_root)])
    )

    proj_own = here.gather_depth(proj_sum.astype(BF16)).reshape(width, -1)
    first_far = far_columns(first_own)
    proj_total = sum_over_group(*row_terms(proj_own, 3, proj_left_root))
    proj_far = far_columns(proj_own)
    own_cols = proj_weight.shape[1]
    proj_grad = jnp.concatenate(
        [
            lax.dynamic_slice_in_dim(part, (2 * q + c) * own_cols, own_cols).T
            for part in proj_far
        ]
    ).astype(F32)
    proj_left_sum = dot_tn(jnp.concatenate(proj_far, axis=1), proj_own)

    def interleave(value):
        value = value.reshape(-1, 1, block)
        zeros = jnp.zeros_like(value)
        return jnp.concatenate(here.by_core(value, zeros), axis=1).reshape(-1)

    head_sums = interleave(jnp.sum(grad_heads.astype(F32), axis=0))
    fc_bias_terms = lax.dynamic_update_slice_in_dim(
        jnp.zeros((hidden,), F32), jnp.sum(grad_pre.astype(F32), axis=0), (2 * q + c) * unit, 0
    )
    vector_terms = jnp.concatenate(
        [
            jnp.sum(grad_normed_one * own_scaled, axis=0),
            jnp.sum(grad_normed_one, axis=0),
            head_sums[:width],
            head_sums[2 * width :],
            jnp.sum(own_branch.astype(F32), axis=0),
            jnp.sum(grad_normed_two * scaled_two, axis=0),
            jnp.sum(grad_normed_two, axis=0),
            fc_bias_terms,
            jnp.sum(grad_top, axis=0),
        ]
    )
    vector_terms = here.after(vector_terms, first_own)
    vector_sum = here.swap_core(vector_terms) + vector_terms
    vector_sum = vector_sum.reshape(depth, -1, 128)
    steps = range(1, depth)
    vector_parts = here.send(
        [lax.dynamic_index_in_dim(vector_sum, (z + k) % depth, 0, False) for k in steps],
        "in",
        [[(n, (n + k) % depth) for n in range(depth)] for k in steps],
    )
    vector_sum = sum(vector_parts, lax.dynamic_index_in_dim(vector_sum, z, 0, False))
    distance = 1
    while distance < plane:
        vector_sum = vector_sum + here.swap_plane([vector_sum], [distance], None)[0]
        distance *= 2
    vector_grad = vector_sum.reshape(-1) * factor

    cut = qkv_cols + out_cols
    first_direction = here.transpose_chips(first_total[:, :cut].astype(BF16), "turn").astype(F32)
    qkv_direction, out_direction = first_direction[:, :qkv_cols], first_direction[:, qkv_cols:]
    qkv_left_sum = first_total[:, cut : cut + out_cols]
    out_left_sum = first_total[:, cut + out_cols :]
    fc_left_sum = fc_total[:, unit_cols:]
    proj_direction = proj_total[: proj_weight.shape[0]]
    proj_right_sum = jnp.concatenate(jnp.split(proj_total[proj_weight.shape[0] :], 2), axis=1)

    fc_right_sum = dot_tn(fc_own, jnp.concatenate(fc_far, axis=1))
    qkv_right_sum = dot_tn(
        first_own[:, :qkv_cols], jnp.concatenate([part[:, :qkv_cols] for part in first_far], axis=1)
    )
    out_right_sum = dot_tn(
        first_own[:, qkv_cols:], jnp.concatenate([part[:, qkv_cols:] for part in first_far], axis=1)
    )

    results = []
    for grad, weight, moment, left, right, found, row_total, col_total in (
        (
            qkv_grad,
            qkv_weight,
            qkv_moment,
            qkv_left,
            qkv_right,
            (qkv_left_sum, qkv_right_sum, qkv_direction),
            width,
            3 * width,
        ),
        (
            out_grad,
            out_weight,
            out_moment,
            out_left,
            out_right,
            (out_left_sum, out_right_sum, out_direction),
            width,
            width,
        ),
        (
            fc_grad,
            fc_weight,
            fc_moment,
            fc_left,
            fc_right,
            (fc_left_sum, fc_right_sum, fc_direction),
            width,
            hidden,
        ),
        (
            proj_grad,
            proj_weight,
            proj_moment,
            proj_left,
            proj_right,
            (proj_left_sum, proj_right_sum, proj_direction),
            hidden,
            width,
        ),
    ):
        left_sum, right_sum, direction = found
        new_moment = MOMENTUM * moment + direction
        new_weight = weight - RATE * new_moment
        results += [
            grad,
            DECAY * left + (1.0 - DECAY) / col_total * left_sum,
            DECAY * right + (1.0 - DECAY) / row_total * right_sum,
            new_moment,
            new_weight,
            new_weight.astype(BF16),
        ]
    new_vector_moment = MOMENTUM * vector_moment + vector_grad
    new_vectors = vectors - RATE * new_vector_moment
    return (output, input_grad, *results, vector_grad, new_vector_moment, new_vectors)


def solution(mesh):
    groups, depth = mesh.shape["grp"], mesh.shape["in"]
    fine = Mesh(mesh.devices.reshape(groups // 4, 2, 2, depth), ALL)
    grp = ("y", "x", "c")
    tokens, cols, rows, flat = P(ALL, None), P("in", grp), P(grp, "in"), P("in")
    matrix_in = (cols, cols, cols, rows, cols, rows)
    matrix_out = (cols, cols, rows, cols, cols, cols)
    return jax.shard_map(
        on_device,
        mesh=fine,
        in_specs=(tokens, tokens, tokens, flat, flat) + matrix_in * 4,
        out_specs=(tokens, tokens) + matrix_out * 4 + (flat, flat, flat),
        check_vma=False,
    )
```
